32 devices in a mesh: segment: 4 (over x, core), vert: 8 (over z, y).
Axes of the slice: x: 2, y: 2, z: 4, core: 2. Of those that a mesh axis runs over, the one named last changes fastest.
Arguments:
- init_feats: bfloat16 [4, 2048, 1024], P(None, 'vert'), may hold values from -6 to 6
- layer_weight: bfloat16 [4, 1024, 1024], P('segment'), may hold values from -0.1875 to 0.1875
- tile_cols: int32 [4, 16], P(None, 'vert'), may hold values from 0 to 1
- tile_vals: bfloat16 [4, 16, 128, 128], P(None, 'vert'), may hold values from -0.5 to 0.5
- send_rows: int32 [4, 64, 8], P(None, 'vert'), may hold values from 0 to 255
- send_count: int32 [4, 64], P(None, 'vert'), may hold values from 1 to 8, as said below
- recv_rows: int32 [4, 64, 8], P(None, 'vert'), may hold values from 0 to 255
- recv_weight: bfloat16 [4, 64, 8], P(None, 'vert'), may hold values from 0.25 to 1
- pair_owner: int32 [4, 2048, 1], P(None, 'vert'), may hold values from 0 to 7; in each aligned block of 256 rows (0 to 255, 256 to 511, ..., all dimensions but the last counted through in order) at most 48 rows name the same one
Outputs:
- losses: float32 [4, 4, 3072], P('segment', None, 'vert')
The draws below stay inside these ranges and needn't reach their ends.
Inputs may be any that keep to these rules, and one draw needn't show every extreme that they name: `send_count`: for every span and sender, each peer gets 1 to 8 used slots and some peer gets exactly 8. `pair_owner`: in each span no device's rows name one owner more than 48 times; some reach 48.
All inputs are finite; a program needn't handle non-finite values.
Results may differ from the reference program's by a relative error of at most 0.0025.
Values may be sent and summed in bfloat16 or wider, within the bound.
No kernel may reach another device: no remote copies, remote signals or barrier semaphores. Data moves between devices by JAX's collectives and lax.ppermute only.
A program may use at most 192 MiB of HBM per device.

```python
import math
import jax
import jax.numpy as jnp
import numpy as np
from jax import lax

HIDDEN_WIDTH = 1024
ROWS = 256
TILE = 128
BCAP = 8
MB = 4
LAYERS = 4
SPAN_ROW_TILES = 2
CAP = 48
VERTS = 2048
N_SEGMENT = 4
N_VERT = 8


def draw_send_count(key, part):
    key = jax.random.fold_in(key, 11)
    first_key, second_key = jax.random.split(key)
    counts = jax.random.randint(first_key, (MB, N_VERT, N_VERT), 1, BCAP + 1)
    picked = jax.random.randint(second_key, (MB, N_VERT, 1), 0, N_VERT)
    filled = jnp.arange(N_VERT)[None, None, :] == picked
    return jnp.where(filled, BCAP, counts).astype(jnp.int32).reshape(MB, N_VERT * N_VERT)


def draw_init_feats(key, part):
    key = jax.random.fold_in(key, 23)
    subkeys = jax.random.split(key, 6)
    groups = 20
    centres = jnp.clip(jax.random.normal(subkeys[0], (MB, groups, HIDDEN_WIDTH), jnp.float32), -4.0, 4.0)
    noise_part = jnp.clip(jax.random.normal(subkeys[1], (MB, VERTS, HIDDEN_WIDTH), jnp.float32), -4.0, 4.0)
    lower_share = 0.45
    upper_share = 0.95
    first_pick = jax.random.randint(subkeys[2], (MB, VERTS), 0, groups)
    second_pick = jax.random.randint(subkeys[3], (MB, VERTS), 0, groups)
    labels = jnp.minimum(first_pick, second_pick)
    blend_share = jax.random.uniform(subkeys[5], (MB, VERTS, 1), jnp.float32, lower_share, upper_share)
    picked = centres[jnp.arange(MB)[:, None], labels]
    values = blend_share * picked + jnp.sqrt(1.0 - blend_share * blend_share) * noise_part
    return values.astype(jnp.bfloat16)


def plant(entries, stream_key, low, high):
    spot = [jax.random.randint(jax.random.fold_in(stream_key, axis), (), 0, length) for axis, length in enumerate(entries.shape)]
    main_axis = entries.shape.index(max(entries.shape))
    neighbour = spot[:main_axis] + [(spot[main_axis] + 1) % entries.shape[main_axis]] + spot[main_axis + 1:]
    return entries.at[tuple(spot)].set(low).at[tuple(neighbour)].set(high)


def steps_of(rng, dims, shards, low, top_value):
    loudness = 1.0
    for axis_at, blocks in shards:
        heights = jax.random.uniform(jax.random.fold_in(jax.random.fold_in(rng, 6), axis_at), (blocks,), jnp.float32, low / len(shards), top_value / len(shards))
        loudness = loudness * jnp.repeat(jnp.exp(heights), dims[axis_at] // blocks).reshape((-1,) + (1,) * (len(dims) - 1 - axis_at))
    return loudness


def shared_out(rng, own, number, rows, count, top, most, skew):
    order = jax.random.permutation(rng, count)
    packed, ordinary = portions_of(count, rows * top, most, skew, True), portions_of(count, rows * top, most, skew, False)
    places = jnp.arange(count)

    def named(sizes, turn):
        used = int((sizes > 0).sum())
        fixed = max(1, used // 4)
        shifted = fixed + (places - fixed + turn * (used - fixed)) % max(1, count - fixed)
        return jnp.zeros((count,), jnp.int32).at[order[jnp.where(places < fixed, places, shifted)]].set(jnp.asarray(sizes, jnp.int32))

    sizes = jnp.where(number % 4 == 0, named(packed, number // 4), named(ordinary, number - number // 4 - 1))
    mixed = jax.random.permutation(jax.random.fold_in(own, 3), count)
    source_of, receiver = mixed[0:count // 2 * 2:2], mixed[1:count // 2 * 2:2]
    margin = jnp.minimum(sizes[source_of] - 1, most - sizes[receiver]) // 2
    margin = jnp.where((source_of == order[0]) | (receiver == order[0]) | (sizes[receiver] == 0), 0, jnp.maximum(margin, 0))
    shifted = jax.random.randint(jax.random.fold_in(own, 4), (count // 2,), 0, 1 << 20) % (margin + 1)
    sizes = sizes.at[source_of].add(-shifted).at[receiver].add(shifted)
    items = jnp.searchsorted(jnp.cumsum(sizes), jnp.arange(rows * top), side="right").astype(jnp.int32)
    listing = items.reshape(top, rows).T
    listing = listing[jax.random.permutation(jax.random.fold_in(own, 1), rows)]
    turn = jax.random.randint(jax.random.fold_in(own, 2), (rows, 1), 0, top)
    return jnp.take_along_axis(listing, (jnp.arange(top)[None, :] + turn) % top, axis=1)


def portions_of(count, total, bound, slope, full):
    weights = [(1 << 20) // math.isqrt(grade ** slope) + 1 for grade in range(1, count + 1)]
    largest = bound if full else min(bound, max(-(-total // count), total * weights[0] // sum(weights)))
    least = 1 if total - largest >= count - 1 else 0
    given, surplus = [largest] + [least] * (count - 1), total - largest - least * (count - 1)
    while surplus > 0:
        movable = [i for i in range(1, count) if given[i] < largest] or [i for i in range(1, count) if given[i] < bound]
        pool, remaining = sum([weights[i] for i in movable]), surplus
        for i in movable:
            addition = min(bound - given[i], max(1, remaining * weights[i] // pool), surplus)
            given[i] = given[i] + addition
            surplus = surplus - addition
    return np.array(given)


def noise(stream_key, dims, spread, bound, cuts=(), dtype=jnp.bfloat16):
    drawn = jax.random.normal(stream_key, dims, jnp.float32) * spread
    if len(cuts) > 0:
        drawn = steps_of(stream_key, dims, cuts, -0.22, 0.18) * drawn
    return jnp.clip(drawn, min=-bound, max=bound).astype(dtype)


def setup_inputs(seed: int = 0) -> dict:
    splits = jax.random.split(jax.random.key(seed), 10)
    init_feats = draw_init_feats(jax.random.fold_in(splits[9], 71), 0)
    layer_weight = noise(splits[1], (LAYERS, HIDDEN_WIDTH, HIDDEN_WIDTH), HIDDEN_WIDTH ** -0.5, 0.1875, ((0, 4),))
    tile_cols = plant(jax.random.randint(splits[2], (MB, N_VERT * SPAN_ROW_TILES), 0, SPAN_ROW_TILES), jax.random.fold_in(splits[2], 1), 0, SPAN_ROW_TILES - 1).astype(jnp.int32)
    tile_vals = noise(splits[3], (MB, N_VERT * SPAN_ROW_TILES, TILE, TILE), TILE ** -0.5, 0.5, ((1, 8),))
    send_rows = plant(jax.random.randint(splits[4], (MB, N_VERT * N_VERT, BCAP), 0, ROWS), jax.random.fold_in(splits[4], 1), 0, ROWS - 1).astype(jnp.int32)
    send_count = draw_send_count(jax.random.fold_in(splits[9], 71), 0)
    recv_rows = plant(jax.random.randint(splits[6], (MB, N_VERT * N_VERT, BCAP), 0, ROWS), jax.random.fold_in(splits[6], 1), 0, ROWS - 1).astype(jnp.int32)
    recv_weight = jnp.clip(0.25 + 0.75 * jax.random.uniform(splits[7], (MB, N_VERT * N_VERT, BCAP), jnp.float32) ** steps_of(splits[7], (MB, N_VERT * N_VERT, BCAP), ((1, 8),), -0.2, 0.2), 0.25, 1.0).astype(jnp.bfloat16)
    pair_owner_keys = jax.random.split(jax.random.fold_in(splits[8], 1), MB * VERTS // ROWS)
    pair_owner_turns = jax.random.permutation(jax.random.fold_in(splits[8], 3), MB * VERTS // ROWS)
    pair_owner = jax.vmap(lambda own, number: shared_out(jax.random.fold_in(splits[8], 2), own, number, ROWS, N_VERT, 1, CAP, 2))(pair_owner_keys, pair_owner_turns).reshape((MB, VERTS, 1))
    return {"init_feats": init_feats, "layer_weight": layer_weight, "tile_cols": tile_cols, "tile_vals": tile_vals, "send_rows": send_rows, "send_count": send_count, "recv_rows": recv_rows, "recv_weight": recv_weight, "pair_owner": pair_owner}


ALPHA_MIX = 0.5
LAMBDA_DECAY = 0.5
SOFTMAX_TEMP = 0.1

def propagate(hidden, init_span, columns, values, srows, scount, rrows, rweight, weight, blend):
    blocks = hidden.reshape(N_VERT, SPAN_ROW_TILES, TILE, HIDDEN_WIDTH)
    picked = blocks[jnp.arange(N_VERT)[:, None], columns.reshape(N_VERT, SPAN_ROW_TILES)]
    local_sum = jnp.einsum('vtij,vtjd->vtid', values.reshape(N_VERT, SPAN_ROW_TILES, TILE, TILE).astype(jnp.float32), picked.astype(jnp.float32)).reshape(N_VERT, ROWS, HIDDEN_WIDTH)
    by_block = hidden.reshape(N_VERT, ROWS, HIDDEN_WIDTH)
    chosen = by_block[jnp.arange(N_VERT)[:, None, None], srows.reshape(N_VERT, N_VERT, BCAP)]
    retain = jnp.arange(BCAP)[None, None, :] < scount.reshape(N_VERT, N_VERT)[:, :, None]
    sent = jnp.where(retain[..., None], chosen, jnp.zeros((), jnp.bfloat16))
    arrived = jnp.swapaxes(sent, 0, 1)
    weighted = arrived.astype(jnp.float32) * rweight.reshape(N_VERT, N_VERT, BCAP, 1).astype(jnp.float32)
    target_rows = rrows.reshape(N_VERT, N_VERT * BCAP)
    border = jnp.zeros((N_VERT, ROWS, HIDDEN_WIDTH), jnp.float32).at[jnp.arange(N_VERT)[:, None], target_rows].add(weighted.reshape(N_VERT, N_VERT * BCAP, HIDDEN_WIDTH))
    mixed = (1.0 - ALPHA_MIX) * (local_sum + border) + ALPHA_MIX * init_span.reshape(N_VERT, ROWS, HIDDEN_WIDTH).astype(jnp.float32)
    support = mixed.astype(jnp.bfloat16).reshape(N_VERT * ROWS, HIDDEN_WIDTH)
    product = jnp.dot(support, weight, preferred_element_type=jnp.float32)
    return jax.nn.relu((1.0 - blend) * support.astype(jnp.float32) + blend * product).astype(jnp.bfloat16)

def rms_unit(vectors):
    vectors = vectors.astype(jnp.float32)
    return (vectors * lax.rsqrt(lax.optimization_barrier(jnp.mean(vectors * vectors, axis=-1, keepdims=True)) + 1e-06)).astype(jnp.bfloat16)

def infonce_loss(embed, init_span, owners):
    target_dev = owners.reshape(N_VERT, ROWS)
    onehot = (target_dev[:, :, None] == jnp.arange(N_VERT)[None, None, :]).astype(jnp.int32)
    before = jnp.cumsum(onehot, axis=1) - onehot
    place = lax.optimization_barrier(jnp.sum(before * onehot, axis=2))
    source = jnp.broadcast_to(jnp.arange(N_VERT)[:, None], (N_VERT, ROWS))
    anchors = jnp.zeros((N_VERT, N_VERT, CAP, HIDDEN_WIDTH), jnp.bfloat16).at[target_dev, source, place].set(embed.reshape(N_VERT, ROWS, HIDDEN_WIDTH))
    keys_all = jnp.zeros((N_VERT, N_VERT, CAP, HIDDEN_WIDTH), jnp.bfloat16).at[target_dev, source, place].set(init_span.reshape(N_VERT, ROWS, HIDDEN_WIDTH))
    live_mask = jnp.zeros((N_VERT, N_VERT, CAP), jnp.float32).at[target_dev, source, place].set(1.0).reshape(N_VERT, N_VERT * CAP)
    query_rows = rms_unit(anchors.reshape(N_VERT, N_VERT * CAP, HIDDEN_WIDTH))
    normalized_keys = rms_unit(keys_all.reshape(N_VERT, N_VERT * CAP, HIDDEN_WIDTH))
    similarity_scores = jnp.einsum('mxq,mwq->mxw', query_rows.astype(jnp.float32), normalized_keys.astype(jnp.float32)) / (HIDDEN_WIDTH * SOFTMAX_TEMP)
    totals = lax.optimization_barrier(jnp.sum(jnp.exp(similarity_scores) * live_mask[:, None, :], axis=2))
    diagonal = jnp.diagonal(similarity_scores, axis1=1, axis2=2)
    result = (jnp.log(totals + 1.0 - live_mask) - diagonal) * live_mask
    return result.reshape(N_VERT * N_VERT * CAP)

def reference(init_feats, layer_weight, tile_cols, tile_vals, send_rows, send_count, recv_rows, recv_weight, pair_owner):
    current = [init_feats[span_id] for span_id in range(MB)]
    per_layer = []
    for layer_id in range(N_SEGMENT):
        mixing = jnp.log(jnp.float32(LAMBDA_DECAY) / jnp.float32(layer_id + 1) + jnp.float32(1.0))
        collected = []
        for span_id in range(MB):
            current[span_id] = propagate(current[span_id], init_feats[span_id], tile_cols[span_id], tile_vals[span_id], send_rows[span_id], send_count[span_id], recv_rows[span_id], recv_weight[span_id], layer_weight[layer_id], mixing)
            collected.append(infonce_loss(current[span_id], init_feats[span_id], pair_owner[span_id]))
        per_layer.append(jnp.stack(collected))
    return jnp.stack(per_layer)
```

```python
import functools

import jax
import jax.numpy as jnp
import numpy as np
from jax import lax
from jax.experimental import pallas as pl
from jax.experimental.pallas import tpu as pltpu
from jax.sharding import PartitionSpec as P

ALPHA_MIX = 0.5
LAMBDA_DECAY = 0.5
SOFTMAX_TEMP = 0.1
NORM_EPS = 1e-06
SPAN_BYTES = 4 * 1024 * 1024


def up_to(count, multiple):
    return -(-count // multiple) * multiple


def swap(block, axis, bit):
    return lax.ppermute(block, axis, [(i, i ^ bit) for i in range(lax.axis_size(axis))])


def rms_unit(vectors):
    scale = lax.rsqrt(jnp.mean(vectors * vectors, axis=-1, keepdims=True) + NORM_EPS)
    return (vectors * scale).astype(jnp.bfloat16)


def encoder_kernel(
    dims, cols_ref, where_ref, pack_ref, spread_ref, pick_ref, live_row_ref, live_col_ref, *rest
):
    layers, blocks, rows, tile, border, slots = dims
    weight_refs = rest[:layers]
    loss_ref, hidden, boundary, anchors, keys, last, weight, weight_sem = rest[layers:]
    width = hidden.shape[-1]
    step = pl.program_id(0)
    phase, block = step // blocks, step % blocks
    row_start = pl.multiple_of(block * rows, rows)
    slot_start = pl.multiple_of(block * slots, slots)
    border_start = pl.multiple_of(block * (border // blocks), border // blocks)

    def fetch(layer, slot):
        for place in range(layers):
            @pl.when(where_ref[layer] == place)
            def _():
                pltpu.make_async_copy(
                    weight_refs[place], weight.at[slot], weight_sem.at[slot]
                ).start()

    def arrive(slot):
        pltpu.make_async_copy(weight_refs[0], weight.at[slot], weight_sem.at[slot]).wait()

    @pl.when(step == 0)
    def _():
        fetch(0, 0)

    init_block = pack_ref[block, pl.ds(0, rows), :]

    def publish(block_out, side, target):
        picked = jnp.dot(pick_ref[0], block_out, preferred_element_type=jnp.float32)
        each = border // blocks
        for receiver in range(blocks):
            boundary[side, receiver, pl.ds(border_start, each), :] = picked[
                receiver * each : (receiver + 1) * each
            ]
        target[pl.ds(slot_start, slots), :] = rms_unit(picked[border:])

    def support_of(side):
        incoming = boundary[side, block].astype(jnp.bfloat16)
        parts = []
        for t in range(rows // tile):
            column = cols_ref[block * (rows // tile) + t]
            start = pl.multiple_of(row_start + column * tile, tile)
            source = jnp.concatenate([hidden[side, pl.ds(start, tile), :], incoming], axis=0)
            parts.append(jnp.dot(spread_ref[t], source, preferred_element_type=jnp.float32))
        gathered = jnp.concatenate(parts, axis=0)
        mixed = (1.0 - ALPHA_MIX) * gathered + ALPHA_MIX * init_block.astype(jnp.float32)
        return mixed.astype(jnp.bfloat16)

    def transform(support, slot, mixing):
        product = jnp.dot(support, weight[slot], preferred_element_type=jnp.float32)
        blended = (1.0 - mixing) * support.astype(jnp.float32) + mixing * product
        return jnp.maximum(blended, 0.0).astype(jnp.bfloat16)

    def score(layer):
        total_slots = blocks * slots
        logits = lax.dot_general(
            keys[...], anchors[...], (((1,), (1,)), ((), ())), preferred_element_type=jnp.float32
        ) / (width * SOFTMAX_TEMP)
        live_row = live_row_ref[...]
        totals = jnp.sum(jnp.exp(logits) * live_col_ref[...], axis=0, keepdims=True)
        key_ids = lax.broadcasted_iota(jnp.int32, (total_slots, total_slots), 0)
        anchor_ids = lax.broadcasted_iota(jnp.int32, (total_slots, total_slots), 1)
        diagonal = jnp.sum(
            jnp.where(key_ids == anchor_ids, logits, 0.0), axis=0, keepdims=True
        )
        loss_ref[pl.ds(layer, 1), :] = (
            jnp.log(totals + 1.0 - live_row) - diagonal
        ) * live_row

    @pl.when(phase == 0)
    def _():
        hidden[0, pl.ds(row_start, rows), :] = init_block
        publish(init_block, 0, keys)

    for layer in range(layers):
        mixing = float(np.log(np.float32(LAMBDA_DECAY) / np.float32(layer + 1) + np.float32(1.0)))
        side, slot = layer % 2, layer % 2

        @pl.when((phase == layer + 1) & (block == 0))
        def _():
            arrive(slot)
            if layer + 1 < layers:
                fetch(layer + 1, 1 - slot)

    mixings = [
        float(np.log(np.float32(LAMBDA_DECAY) / np.float32(layer + 1) + np.float32(1.0)))
        for layer in range(layers)
    ]

    @pl.when((phase > 0) & (phase < layers))
    def _():
        layer = phase - 1
        side = layer % 2
        mixing = jnp.float32(mixings[0])
        for index in range(1, layers):
            mixing = jnp.where(layer == index, jnp.float32(mixings[index]), mixing)
        support = support_of(side)
        block_out = transform(support, side, mixing)
        hidden[1 - side, pl.ds(row_start, rows), :] = block_out
        publish(block_out, 1 - side, anchors)

        @pl.when(block == blocks - 1)
        def _():
            score(layer)

    @pl.when(phase == layers)
    def _():
        side = (layers - 1) % 2
        support = support_of(side)
        chosen = jnp.dot(pick_ref[0, border:, :], support, preferred_element_type=jnp.float32)
        last[pl.ds(slot_start, slots), :] = chosen.astype(jnp.bfloat16)

        @pl.when(block == blocks - 1)
        def _():
            final = transform(last[...], side, mixings[layers - 1])
            anchors[...] = rms_unit(final.astype(jnp.float32))
            score(layers - 1)


def encode(pack, weights, where, cols, spread, pick, live, rows, tile, border, slots):
    layers = len(weights)
    blocks, _, width = pack.shape
    tiles = rows // tile
    total = blocks * slots
    dims = (layers, blocks, rows, tile, border, slots)
    block_of = lambda i, *_: (i % blocks, 0, 0)
    whole = lambda *shape: pl.BlockSpec(
        shape, lambda i, *_: (0,) * len(shape), pipeline_mode=pl.Buffered(1)
    )
    return pl.pallas_call(
        functools.partial(encoder_kernel, dims),
        out_shape=jax.ShapeDtypeStruct((layers, total), jnp.float32),
        grid_spec=pltpu.PrefetchScalarGridSpec(
            num_scalar_prefetch=2,
            grid=((layers + 1) * blocks,),
            in_specs=[
                whole(*pack.shape),
                pl.BlockSpec((tiles, tile, spread.shape[-1]), block_of),
                pl.BlockSpec((1, border + slots, rows), block_of),
                whole(1, total),
                whole(total, 1),
            ]
            + [pl.BlockSpec(memory_space=pl.ANY)] * layers,
            out_specs=pl.BlockSpec((layers, total), lambda i, *_: (0, 0)),
            scratch_shapes=[
                pltpu.VMEM((2, blocks * rows, width), jnp.bfloat16),
                pltpu.VMEM((2, blocks, border, width), jnp.float32),
                pltpu.VMEM((total, width), jnp.bfloat16),
                pltpu.VMEM((total, width), jnp.bfloat16),
                pltpu.VMEM((total, width), jnp.bfloat16),
                pltpu.VMEM((2, width, width), jnp.bfloat16),
                pltpu.SemaphoreType.DMA((2,)),
            ],
        ),
        compiler_params=pltpu.CompilerParams(vmem_limit_bytes=48 * 1024 * 1024),
        cost_estimate=pl.CostEstimate(
            flops=2 * layers * blocks * rows * width * width,
            bytes_accessed=2 * layers * width * width + 2 * pack.size,
            transcendentals=layers * total * total,
        ),
    )(cols, where, pack, spread, pick, live[None, :], live[:, None], *weights)


def local(
    init_feats,
    layer_weight,
    tile_cols,
    tile_vals,
    send_rows,
    send_count,
    recv_rows,
    recv_weight,
    pair_owner,
):
    segment_count = lax.axis_size("segment")
    vert_count = lax.axis_size("vert")
    position = lax.axis_index("segment")
    mine = lax.axis_index("vert")
    span_count, row_count, width = init_feats.shape
    capacity = 3 * row_count // (2 * vert_count)
    slots = up_to(capacity, 16)
    tile_size = tile_vals.shape[-1]
    tiles = row_count // tile_size
    slot_count = send_rows.shape[-1]
    border = vert_count * slot_count
    span = position % span_count
    bf16 = jnp.bfloat16

    def of_span(array):
        return lax.dynamic_index_in_dim(array, span, 0, keepdims=False)

    small = [send_rows, recv_rows, send_count, tile_cols, pair_owner, recv_weight]
    small = [of_span(array).reshape(-1).astype(bf16) for array in small]
    sizes = [array.shape[0] for array in small]
    ends = [sum(sizes[: i + 1]) for i in range(len(sizes))]
    adjacency_rows = tiles * tile_size * tile_size // width
    small_rows = up_to(-(-ends[-1] // width), 16)
    small = jnp.concatenate(small + [jnp.zeros((small_rows * width - ends[-1],), bf16)])
    pack = jnp.concatenate(
        [
            of_span(init_feats),
            of_span(tile_vals).reshape(adjacency_rows, width),
            small.reshape(small_rows, width),
        ]
    )
    pack = lax.all_gather(pack, "vert", axis=0, tiled=False)

    weights = [layer_weight[0]]
    reach = 1
    while reach < segment_count:
        weights = weights + [swap(w, "segment", reach) for w in weights]
        reach *= 2
    where = jnp.arange(segment_count, dtype=jnp.int32) ^ position

    tables = pack[:, row_count + adjacency_rows :, :].reshape(vert_count, -1)
    starts = [0] + ends
    tables = [tables[:, starts[i] : ends[i]] for i in range(len(sizes))]
    ints = [table.astype(jnp.int32) for table in tables[:-1]]
    all_send, all_recv, all_count, all_cols, all_owner = ints
    row_ids = jnp.arange(row_count, dtype=jnp.int32)
    used = jnp.arange(slot_count)[None, None, :] < all_count[:, :, None]
    used = used.reshape(vert_count, border)
    sends = used[:, :, None] & (all_send[:, :, None] == row_ids)
    owned = all_owner == mine
    place = jnp.cumsum(owned.astype(jnp.int32), axis=1) - 1
    fills = owned[:, None, :] & (
        place[:, None, :] == jnp.arange(slots, dtype=jnp.int32)[None, :, None]
    )
    pick = jnp.concatenate([sends, fills], axis=1).astype(bf16)
    live = jnp.any(fills, axis=2).astype(jnp.float32).reshape(-1)
    placing = jnp.where(
        all_recv[:, None, :] == row_ids[None, :, None], tables[-1][:, None, :], jnp.zeros((), bf16)
    )
    adjacency = pack[:, row_count : row_count + adjacency_rows, :]
    adjacency = adjacency.reshape(vert_count * tiles, tile_size, tile_size)
    spread = jnp.concatenate(
        [adjacency, placing.reshape(vert_count * tiles, tile_size, border)], axis=2
    )
    losses = encode(
        pack, weights, where, all_cols.reshape(-1), spread, pick, live,
        row_count, tile_size, border, slots,
    )
    losses = losses.reshape(segment_count, vert_count, slots)[:, :, :capacity]
    losses = losses.reshape(segment_count, -1)
    losses = lax.all_to_all(losses, "segment", split_axis=0, concat_axis=0, tiled=True)
    return losses[None, :span_count]


def from_behind(block, axis, distance):
    devices = range(lax.axis_size(axis))
    route = [(i - distance, i) for i in devices if i - distance in devices]
    return lax.ppermute(block, axis, route)


def rms_rows(vectors):
    vectors = vectors.astype(jnp.float32)
    return (
        vectors * lax.rsqrt(jnp.mean(vectors * vectors, axis=-1, keepdims=True) + 1e-06)
    ).astype(jnp.bfloat16)


def pack_pairs(owners, embed, init_span, capacity, vert_count):
    row_count = embed.shape[0]
    target_dev = owners[:, 0]
    onehot = (target_dev[:, None] == jnp.arange(vert_count)[None, :]).astype(jnp.int32)
    before = jnp.cumsum(onehot, axis=0) - onehot
    place = jnp.sum(before * onehot, axis=1)
    lookup = (
        jnp.full((vert_count * capacity,), row_count, jnp.int32)
        .at[target_dev * capacity + place]
        .set(jnp.arange(row_count, dtype=jnp.int32))
    )
    blank = jnp.zeros((1, embed.shape[1]), jnp.bfloat16)
    padded_embed = jnp.concatenate([embed, blank], axis=0)
    padded_init = jnp.concatenate([init_span, blank], axis=0)
    anchors = padded_embed[lookup].reshape(vert_count, capacity, -1)
    keys_all = padded_init[lookup].reshape(vert_count, capacity, -1)
    flags = (lookup < row_count).astype(jnp.bfloat16).reshape(vert_count, capacity)
    return (anchors, keys_all, flags)


def score_pairs(anchors, keys_all, flags):
    feature_columns = anchors.shape[-1]
    query_rows = rms_rows(anchors.reshape(-1, feature_columns))
    normalized_keys = rms_rows(keys_all.reshape(-1, feature_columns))
    similarity_scores = jnp.dot(
        query_rows, normalized_keys.T, preferred_element_type=jnp.float32
    ) / (feature_columns * SOFTMAX_TEMP)
    live_mask = flags.reshape(-1).astype(jnp.float32)
    totals = jnp.sum(jnp.exp(similarity_scores) * live_mask[None, :], axis=1)
    diagonal = jnp.diagonal(similarity_scores)
    return (jnp.log(totals + 1.0 - live_mask) - diagonal) * live_mask


def local_by_section(
    init_feats,
    layer_weight,
    tile_cols,
    tile_vals,
    send_rows,
    send_count,
    recv_rows,
    recv_weight,
    pair_owner,
):
    segment_count = lax.axis_size("segment")
    vert_count = lax.axis_size("vert")
    position = lax.axis_index("segment")
    span_count, row_count, feature_columns = init_feats.shape
    capacity = 3 * row_count // (2 * vert_count)
    tile_size = tile_vals.shape[-1]
    tile_rows = row_count // tile_size
    slot_count = send_rows.shape[-1]
    weight = layer_weight[0]
    mixing = jnp.log(LAMBDA_DECAY / (position.astype(jnp.float32) + 1.0) + 1.0)
    row_ids = jnp.arange(row_count, dtype=jnp.int32)

    def section(span_id, hidden, init_span):
        columns = tile_cols[span_id]
        values = tile_vals[span_id]
        picked = hidden.reshape(tile_rows, tile_size, feature_columns)[columns]
        local_sum = jnp.einsum(
            "tij,tjd->tid", values, picked, preferred_element_type=jnp.float32
        ).reshape(row_count, feature_columns)
        retain = jnp.arange(slot_count)[None, :] < send_count[span_id][:, None]
        outgoing = jnp.where(
            retain[..., None], hidden[send_rows[span_id]], jnp.zeros((), jnp.bfloat16)
        )
        incoming = lax.all_to_all(outgoing, "vert", split_axis=0, concat_axis=0, tiled=True)
        targets = recv_rows[span_id].reshape(-1)
        edge_weights = recv_weight[span_id].reshape(-1)
        placing = jnp.where(
            targets[None, :] == row_ids[:, None], edge_weights[None, :], jnp.zeros((), jnp.bfloat16)
        )
        border = jnp.dot(
            placing, incoming.reshape(-1, feature_columns), preferred_element_type=jnp.float32
        )
        mixed = (1.0 - ALPHA_MIX) * (local_sum + border) + ALPHA_MIX * init_span.astype(jnp.float32)
        support = mixed.astype(jnp.bfloat16)
        product = jnp.dot(support, weight, preferred_element_type=jnp.float32)
        return jax.nn.relu((1.0 - mixing) * support.astype(jnp.float32) + mixing * product).astype(
            jnp.bfloat16
        )

    stored = jnp.zeros((span_count, row_count, feature_columns), jnp.bfloat16)

    def advance(moment, carry):
        arrived, stored_now = carry
        span_raw = moment - position
        active = (span_raw >= 0) & (span_raw < span_count)
        span_id = jnp.clip(span_raw, 0, span_count - 1)
        init_span = init_feats[span_id]
        hidden = jnp.where(position == 0, init_span, arrived)
        result = section(span_id, hidden, init_span)
        passed = from_behind(result, "segment", 1)
        stored_now = jnp.where(active, stored_now.at[span_id].set(result), stored_now)
        return (passed, stored_now)

    start_carry = (jnp.zeros((row_count, feature_columns), jnp.bfloat16), stored)
    final_carry = lax.fori_loop(0, span_count + segment_count - 1, advance, start_carry)
    stored = final_carry[1]

    def pack_one(owners, embed, init_span):
        return pack_pairs(owners, embed, init_span, capacity, vert_count)

    anchors, keys_all, flags = jax.vmap(pack_one)(pair_owner, stored, init_feats)
    got_anchors, got_keys, got_flags = (
        lax.all_to_all(anchors, "vert", split_axis=1, concat_axis=1, tiled=True),
        lax.all_to_all(keys_all, "vert", split_axis=1, concat_axis=1, tiled=True),
        lax.all_to_all(flags, "vert", split_axis=1, concat_axis=1, tiled=True),
    )
    losses = jax.vmap(score_pairs)(got_anchors, got_keys, got_flags)
    return losses[None]


def solution(mesh):
    def run(init_feats, *rest):
        fits = mesh.shape["vert"] * init_feats[0].size * 2 <= SPAN_BYTES
        plan = local if fits and init_feats.shape[0] <= mesh.shape["segment"] else local_by_section
        return plan(init_feats, *rest)

    return jax.shard_map(
        run,
        mesh=mesh,
        in_specs=(
            P(None, "vert", None),
            P("segment", None, None),
            P(None, "vert"),
            P(None, "vert", None, None),
            P(None, "vert", None),
            P(None, "vert"),
            P(None, "vert", None),
            P(None, "vert", None),
            P(None, "vert", None),
        ),
        out_specs=P("segment", None, "vert"),
        check_vma=False,
    )
```

```python
import functools
import itertools

import jax
import jax.numpy as jnp
import numpy as np
from jax import lax
from jax.experimental import pallas as pl
from jax.experimental.pallas import tpu as pltpu
from jax.sharding import Mesh
from jax.sharding import PartitionSpec as P

ALPHA_MIX = 0.5
LAMBDA_DECAY = 0.5
SOFTMAX_TEMP = 0.1
NORM_EPS = 1e-06

AXES = ("x", "core", "zh", "zl", "y")
SPANS, SEGMENTS, VERTS = 4, 4, 8
SMALL_ROWS = 16
LANES = 128
SEND, RECV, WEIGHT, COLS, OWNER = 0, 128, 256, 512, 640


def exchange(block, axis, core=None):
    sizes = [range(lax.axis_size(name)) for name in AXES]
    at = AXES.index(axis)
    pairs = []
    for index, here in enumerate(itertools.product(*sizes)):
        there = list(here)
        there[at] = 1 - there[at]
        target = functools.reduce(lambda total, digit: total * 2 + digit, there, 0)
        if core is None or here[1] == core:
            pairs.append((index, target))
    return lax.ppermute(block, AXES, pairs)


def rms_unit(vectors):
    scale = lax.rsqrt(jnp.mean(vectors * vectors, axis=-1, keepdims=True) + NORM_EPS)
    return (vectors * scale).astype(jnp.bfloat16)


def mixing_of(layer):
    return float(np.log(np.float32(LAMBDA_DECAY) / np.float32(layer + 1) + np.float32(1.0)))


def turned(matrix):
    rows, columns = matrix.shape
    whole = jnp.concatenate([matrix, jnp.zeros((rows, LANES - columns), matrix.dtype)], axis=1)
    return jnp.transpose(whole)[:columns]


def pack_kernel(
    place_ref, init_ref, tiles_ref, send_ref, count_ref, recv_ref, weight_ref, cols_ref, owner_ref,
    mine_ref, other_ref, small, sems,
):
    x, core, zh = place_ref[0], place_ref[1], place_ref[2]
    half, width = mine_ref.shape[0] - SMALL_ROWS, init_ref.shape[-1]
    peers, slots = send_ref.shape[1:]
    tiles, rows = cols_ref.shape[-1], owner_ref.shape[-1]
    first = pl.multiple_of(core * half, half)
    spans = (zh * 2 + x, (1 - zh) * 2 + x)
    copies = []
    for i, out_ref in enumerate((mine_ref, other_ref)):
        copies.append(
            pltpu.make_async_copy(
                init_ref.at[spans[i], pl.ds(first, half), :],
                out_ref.at[pl.ds(0, half), pl.ds(0, width)],
                sems.at[2 * i],
            )
        )
        copies.append(
            pltpu.make_async_copy(
                tiles_ref.at[spans[i], core],
                out_ref.at[pl.ds(0, half), pl.ds(width, half)],
                sems.at[2 * i + 1],
            )
        )
    for copy in copies:
        copy.start()
    small[...] = jnp.zeros_like(small)
    for i, out_ref in enumerate((mine_ref, other_ref)):
        span = spans[i]
        sends = turned(send_ref[span].astype(jnp.float32))
        used = lax.broadcasted_iota(jnp.int32, (slots, peers), 0) < count_ref[pl.ds(span, 1), :]
        small[i, 0:slots, SEND : SEND + peers] = jnp.where(used, sends, float(rows))
        small[i, 0:slots, RECV : RECV + peers] = turned(recv_ref[span].astype(jnp.float32))
        small[i, 0:slots, WEIGHT : WEIGHT + peers] = turned(weight_ref[span].astype(jnp.float32))
        small[i, 0:1, COLS : COLS + tiles] = cols_ref[pl.ds(span, 1), :].astype(jnp.float32)
        small[i, 0:1, OWNER : OWNER + rows] = owner_ref[pl.ds(span, 1), :].astype(jnp.float32)
        out_ref[half : half + SMALL_ROWS, :] = small[i].astype(jnp.bfloat16)
    for copy in copies:
        copy.wait()


def support_of(block, spread_ref, cols_ref, init_ref, hidden, boundary):
    tile = spread_ref.shape[1]
    rows = init_ref.shape[1]
    incoming = boundary[block].astype(jnp.bfloat16)
    depth = tile + incoming.shape[0]
    parts = []
    for t in range(rows // tile):
        column = cols_ref[block, t]
        start = pl.multiple_of(column * tile, tile)
        source = jnp.concatenate([hidden[block, pl.ds(start, tile), :], incoming], axis=0)
        gathered = jnp.dot(
            spread_ref[block * (rows // tile) + t, :, 0:depth],
            source,
            preferred_element_type=jnp.float32,
        )
        init = init_ref[block, t * tile : (t + 1) * tile, :].astype(jnp.float32)
        parts.append(((1.0 - ALPHA_MIX) * gathered + ALPHA_MIX * init).astype(jnp.bfloat16))
    return jnp.concatenate(parts, axis=0)


def transform(support, weight, mixing):
    product = jnp.dot(support, weight, preferred_element_type=jnp.float32)
    blended = (1.0 - mixing) * support.astype(jnp.float32) + mixing * product
    return jnp.maximum(blended, 0.0).astype(jnp.bfloat16)


def publish(block, block_out, pick_ref, boundary, target):
    receivers, border, _ = boundary.shape
    each = border // receivers
    picked = jnp.dot(pick_ref[block], block_out, preferred_element_type=jnp.float32)
    border_start = pl.multiple_of(block * each, each)
    for receiver in range(receivers):
        boundary[receiver, pl.ds(border_start, each), :] = picked[
            receiver * each : (receiver + 1) * each
        ]
    slots = target.shape[0] // receivers
    slot_start = pl.multiple_of(block * slots, slots)
    target[pl.ds(slot_start, slots), :] = rms_unit(picked[border:])


def score(keys, anchors, live_ref):
    total, width = keys.shape
    logits = lax.dot_general(
        keys[...], anchors[...], (((1,), (1,)), ((), ())), preferred_element_type=jnp.float32
    ) / (width * SOFTMAX_TEMP)
    live = live_ref[:, 0:1]
    key_ids = lax.broadcasted_iota(jnp.int32, (total, total), 0)
    anchor_ids = lax.broadcasted_iota(jnp.int32, (total, total), 1)
    same = key_ids == anchor_ids
    live_row = jnp.sum(jnp.where(same, live, 0.0), axis=0, keepdims=True)
    totals = jnp.sum(jnp.exp(logits) * live, axis=0, keepdims=True)
    diagonal = jnp.sum(jnp.where(same, logits, 0.0), axis=0, keepdims=True)
    return (jnp.log(totals + 1.0 - live_row) - diagonal) * live_row


def run_layer(spread_ref, cols_ref, init_ref, pick_ref, source, border_in, weight, mixing,
              target, border_out, anchors, group=2, unroll=4):
    blocks, rows, _ = init_ref.shape

    def advance(chunk, carry):
        support = jnp.concatenate(
            [
                support_of(chunk * group + k, spread_ref, cols_ref, init_ref, source, border_in)
                for k in range(group)
            ],
            axis=0,
        )
        out = transform(support, weight[...], mixing)
        for k in range(group):
            block_out = out[k * rows : (k + 1) * rows]
            target[chunk * group + k] = block_out
            publish(chunk * group + k, block_out, pick_ref, border_out, anchors)
        return carry

    lax.fori_loop(0, blocks // group, advance, 0, unroll=unroll)


def first_kernel(
    place_ref, init_feats, tile_vals, mine_ref, *rest
):
    blocks = VERTS
    nets, flips = rest[: blocks - 1], rest[blocks - 1 : 2 * blocks - 2]
    weights = rest[2 * blocks - 2 : 2 * blocks + 2]
    (init_ref, spread_ref, pick_ref, cols_out, live_ref, keys, hidden, boundary, loss_ref,
     boundary0, anchors, small, weight, cols_ref, sems, weight_sems) = rest[2 * blocks + 2 :]
    x, core, zh, zl, y = [place_ref[i] for i in range(5)]
    vert = zh * 4 + zl * 2 + y
    rows, width = init_ref.shape[1:]
    half = rows // 2
    tile = spread_ref.shape[1]
    tiles = rows // tile
    border = boundary.shape[1]
    each = border // blocks
    slots = keys.shape[0] // blocks

    def start(source, target, sem):
        copy = pltpu.make_async_copy(source, target, sem)
        copy.start()
        return copy

    for place, source in enumerate(weights):
        by_x, by_core = place // 2, place % 2

        @pl.when((x == by_x) & (core == by_core))
        def _():
            pltpu.make_async_copy(source, weight, weight_sems.at[0]).start()

    span = zh * 2 + x
    copies = [
        start(init_feats.at[span], init_ref.at[vert], sems.at[0]),
        start(mine_ref.at[pl.ds(half, SMALL_ROWS), :], small.at[vert], sems.at[1]),
    ]
    at = 2
    for t in range(tiles):
        target = spread_ref.at[vert * tiles + t, :, pl.ds(0, tile)]
        copies.append(start(tile_vals.at[span, t], target, sems.at[at]))
        at += 1
    for k in range(1, blocks):
        block = vert ^ k
        for part, source in ((core, nets[k - 1]), (1 - core, flips[k - 1])):
            first = pl.multiple_of(part * half, half)
            copies.append(
                start(
                    source.at[pl.ds(0, half), pl.ds(0, width)],
                    init_ref.at[block, pl.ds(first, half), :],
                    sems.at[at],
                )
            )
            copies.append(
                start(
                    source.at[pl.ds(0, half), pl.ds(width, tile)],
                    spread_ref.at[block * tiles + part, :, pl.ds(0, tile)],
                    sems.at[at + 1],
                )
            )
            at += 2
        source = nets[k - 1].at[pl.ds(half, SMALL_ROWS), :]
        copies.append(start(source, small.at[block], sems.at[at]))
        at += 1
    for copy in copies:
        copy.wait()

    owner = core * 4 + zl * 2 + y
    tables = [small[block].astype(jnp.float32) for block in range(blocks)]
    owners = jnp.concatenate([table[0:1, OWNER : OWNER + rows] for table in tables], axis=0)
    cols_out[...] = jnp.concatenate(
        [table[0:1, COLS : COLS + LANES] for table in tables], axis=0
    ).astype(jnp.int32)
    to_scalar = start(cols_out, cols_ref, sems.at[at])
    owned = jnp.where(owners == owner.astype(jnp.float32), 1.0, 0.0)
    earlier = lax.broadcasted_iota(jnp.int32, (rows, rows), 0) < lax.broadcasted_iota(
        jnp.int32, (rows, rows), 1
    )
    rank = jnp.dot(
        owned.astype(jnp.bfloat16),
        jnp.where(earlier, 1.0, 0.0).astype(jnp.bfloat16),
        preferred_element_type=jnp.float32,
    )
    row_ids = lax.broadcasted_iota(jnp.int32, (each, rows), 1).astype(jnp.float32)
    slot_ids = lax.broadcasted_iota(jnp.int32, (slots, rows), 0).astype(jnp.float32)
    for block in range(blocks):
        table = tables[block]
        sends = [
            jnp.where(table[0:each, SEND + peer : SEND + peer + 1] == row_ids, 1.0, 0.0)
            for peer in range(blocks)
        ]
        fills = jnp.where(
            slot_ids == rank[block : block + 1], owned[block : block + 1], 0.0
        )
        pick_ref[block] = jnp.concatenate(sends + [fills], axis=0).astype(jnp.bfloat16)
        live_ref[block * slots : (block + 1) * slots, :] = jnp.broadcast_to(
            jnp.sum(fills, axis=1, keepdims=True), (slots, LANES)
        )
        placing = [
            jnp.where(
                table[0:each, RECV + peer : RECV + peer + 1] == row_ids,
                table[0:each, WEIGHT + peer : WEIGHT + peer + 1],
                0.0,
            )
            for peer in range(blocks)
        ]
        placing = jnp.concatenate(
            placing + [jnp.zeros((LANES - border, rows), jnp.float32)], axis=0
        )
        placing = jnp.transpose(placing).astype(jnp.bfloat16)
        for t in range(tiles):
            spread_ref[block * tiles + t, :, tile : tile + LANES] = placing[
                t * tile : (t + 1) * tile
            ]

    def begin(block, carry):
        publish(block, init_ref[block], pick_ref, boundary0, keys)
        return carry

    lax.fori_loop(0, blocks, begin, 0, unroll=4)
    to_scalar.wait()
    pltpu.make_async_copy(weights[0], weight, weight_sems.at[0]).wait()
    run_layer(
        spread_ref, cols_ref, init_ref, pick_ref, init_ref, boundary0, weight, mixing_of(0),
        hidden, boundary, anchors,
    )
    loss_ref[...] = score(keys, anchors, live_ref)


def rest_kernel(
    place_ref, cols_ref, init_ref, spread_ref, pick_ref, live_ref, keys, hidden, boundary,
    loss0_ref, own_ref, flip_ref, even_ref, even_flip_ref, odd_ref, odd_other_ref,
    odd_flip_ref, odd_other_flip_ref, loss_ref, held, border_held, anchors, last, weight,
    weight_sems,
):
    x, core, zl = place_ref[0], place_ref[1], place_ref[3]
    layers = SEGMENTS
    blocks = init_ref.shape[0]
    slots = keys.shape[0] // blocks
    half = weight.shape[1] // 2

    def fetch(layer):
        slot, by_x, by_core = layer % 2, layer // 2, layer % 2

        def load(source, part, to):
            first = part * half if isinstance(part, int) else pl.multiple_of(part * half, half)
            pltpu.make_async_copy(
                source, weight.at[slot, pl.ds(first, half), :], weight_sems.at[slot, to]
            ).start()

        def load_whole(source):
            for part in range(2):
                load(source.at[pl.ds(part * half, half), :], part, part)

        near = x == by_x
        pl.when(near & (core == by_core))(lambda: load_whole(own_ref))
        pl.when(near & (core != by_core))(lambda: load_whole(flip_ref))
        if by_core == 0:
            pl.when((x != by_x) & (core == 0))(lambda: load_whole(even_ref))
            pl.when((x != by_x) & (core == 1))(lambda: load_whole(even_flip_ref))
        else:

            @pl.when((x != by_x) & (core == 1))
            def _():
                load(odd_ref, zl, 0)
                load(odd_other_ref, 1 - zl, 1)

            @pl.when((x != by_x) & (core == 0))
            def _():
                load(odd_flip_ref, zl, 0)
                load(odd_other_flip_ref, 1 - zl, 1)

    def arrive(layer):
        slot = layer % 2
        for part in range(2):
            pltpu.make_async_copy(
                own_ref.at[pl.ds(part * half, half), :],
                weight.at[slot, pl.ds(part * half, half), :],
                weight_sems.at[slot, part],
            ).wait()

    fetch(1)

    def report(layer, losses):
        for copy in range(2):
            loss_ref[2 * layer + copy : 2 * layer + copy + 1, :] = losses

    report(0, loss0_ref[...])
    source, border_in = hidden, boundary
    for layer in range(1, layers - 1):
        arrive(layer)
        fetch(layer + 1)
        target, border_out = held.at[layer % 2], border_held.at[layer % 2]
        run_layer(
            spread_ref, cols_ref, init_ref, pick_ref, source, border_in, weight.at[layer % 2],
            mixing_of(layer), target, border_out, anchors,
        )
        report(layer, score(keys, anchors, live_ref))
        source, border_in = target, border_out

    border = boundary.shape[1]

    def choose(block, carry):
        support = support_of(block, spread_ref, cols_ref, init_ref, source, border_in)
        chosen = jnp.dot(pick_ref[block, border:, :], support, preferred_element_type=jnp.float32)
        slot_start = pl.multiple_of(block * slots, slots)
        last[pl.ds(slot_start, slots), :] = chosen.astype(jnp.bfloat16)
        return carry

    lax.fori_loop(0, blocks, choose, 0, unroll=4)
    arrive(layers - 1)
    final = transform(last[...], weight[(layers - 1) % 2], mixing_of(layers - 1))
    anchors[...] = rms_unit(final.astype(jnp.float32))
    report(layers - 1, score(keys, anchors, live_ref))


VMEM = pl.BlockSpec(memory_space=pltpu.VMEM)
SMEM = pl.BlockSpec(memory_space=pltpu.SMEM)
HBM = pl.BlockSpec(memory_space=pltpu.HBM)
VMEM_LIMIT = 40 * 1024 * 1024


def local(
    init_feats,
    layer_weight,
    tile_cols,
    tile_vals,
    send_rows,
    send_count,
    recv_rows,
    recv_weight,
    pair_owner,
):
    span_count, rows, width = init_feats.shape
    tile = tile_vals.shape[-1]
    tiles = rows // tile
    blocks = VERTS
    border = blocks * send_rows.shape[-1]
    slots = 3 * rows // (2 * blocks)
    total = blocks * slots
    half = rows // 2
    bf16, f32 = jnp.bfloat16, jnp.float32
    shape = jax.ShapeDtypeStruct
    zh, zl = lax.axis_index("zh"), lax.axis_index("zl")
    place = jnp.stack([lax.axis_index(name) for name in AXES]).astype(jnp.int32)
    own = layer_weight[0]
    odd_part = lax.dynamic_slice(own, (zl * (width // 2), 0), (width // 2, width))

    packed = shape((half + SMALL_ROWS, width + tile), bf16)
    mine, other = pl.pallas_call(
        pack_kernel,
        out_shape=(packed, packed),
        in_specs=[SMEM, HBM, HBM] + [VMEM] * 6,
        out_specs=(VMEM, VMEM),
        scratch_shapes=[
            pltpu.VMEM((2, SMALL_ROWS, width + tile), f32),
            pltpu.SemaphoreType.DMA((4,)),
        ],
    )(
        place, init_feats, tile_vals, send_rows, send_count, recv_rows, recv_weight, tile_cols,
        pair_owner[:, :, 0],
    )

    even = exchange(own, "x", core=0)
    odd = exchange(odd_part, "x", core=1)
    net = {4: exchange(other, "zh"), 2: exchange(mine, "zl"), 1: exchange(mine, "y")}
    net[3] = exchange(net[2], "y")
    net[6] = exchange(net[4], "zl")
    net[5] = exchange(net[4], "y")
    net[7] = exchange(net[6], "y")
    flip = exchange(own, "core")
    flips = {k: exchange(net[k], "core") for k in net}
    odd_other = exchange(odd, "zl", core=1)
    odd_flip = exchange(odd, "core", core=1)
    even_flip = exchange(even, "core", core=0)
    odd_other_flip = exchange(odd_other, "core", core=1)

    keep = [
        shape((blocks, rows, width), bf16),
        shape((blocks * tiles, tile, tile + LANES), bf16),
        shape((blocks, border + slots, rows), bf16),
        shape((blocks, LANES), jnp.int32),
        shape((total, LANES), f32),
        shape((total, width), bf16),
        shape((blocks, rows, width), bf16),
        shape((blocks, border, width), f32),
        shape((1, total), f32),
    ]
    order = range(1, blocks)
    init, spread, pick, cols, live, keys, hidden, boundary, loss0 = pl.pallas_call(
        first_kernel,
        out_shape=keep,
        in_specs=[SMEM] + [HBM] * (3 + 2 * (blocks - 1) + 4),
        out_specs=[VMEM] * len(keep),
        scratch_shapes=[
            pltpu.VMEM((blocks, border, width), f32),
            pltpu.VMEM((total, width), bf16),
            pltpu.VMEM((blocks, SMALL_ROWS, width + tile), bf16),
            pltpu.VMEM((width, width), bf16),
            pltpu.SMEM((blocks, LANES), jnp.int32),
            pltpu.SemaphoreType.DMA((8 * blocks,)),
            pltpu.SemaphoreType.DMA((1,)),
        ],
        compiler_params=pltpu.CompilerParams(vmem_limit_bytes=VMEM_LIMIT),
        cost_estimate=pl.CostEstimate(
            flops=2 * blocks * rows * width * width, bytes_accessed=1 << 24, transcendentals=0
        ),
    )(
        place, init_feats, tile_vals, mine, *[net[k] for k in order], *[flips[k] for k in order],
        own, flip, even, even_flip,
    )
    losses = pl.pallas_call(
        rest_kernel,
        out_shape=shape((2 * SEGMENTS, total), f32),
        in_specs=[SMEM, SMEM] + [VMEM] * 8 + [HBM] * 8,
        out_specs=VMEM,
        scratch_shapes=[
            pltpu.VMEM((2, blocks, rows, width), bf16),
            pltpu.VMEM((2, blocks, border, width), f32),
            pltpu.VMEM((total, width), bf16),
            pltpu.VMEM((total, width), bf16),
            pltpu.VMEM((2, width, width), bf16),
            pltpu.SemaphoreType.DMA((2, 2)),
        ],
        compiler_params=pltpu.CompilerParams(vmem_limit_bytes=VMEM_LIMIT),
        cost_estimate=pl.CostEstimate(
            flops=6 * blocks * rows * width * width, bytes_accessed=1 << 24, transcendentals=0
        ),
    )(
        place, cols, init, spread, pick, live, keys, hidden, boundary, loss0, own, flip, even,
        even_flip, odd, odd_other, odd_flip, odd_other_flip,
    )
    losses = lax.all_to_all(losses, ("x", "core", "zh"), split_axis=0, concat_axis=0, tiled=True)
    losses = lax.dynamic_index_in_dim(
        losses.reshape(2, 2, 2, total), zh, axis=1, keepdims=False
    )
    return jnp.swapaxes(losses, 0, 1).reshape(1, span_count, total)


def from_behind(block, axis, distance):
    devices = range(lax.axis_size(axis))
    route = [(i - distance, i) for i in devices if i - distance in devices]
    return lax.ppermute(block, axis, route)


def rms_rows(vectors):
    vectors = vectors.astype(jnp.float32)
    return (
        vectors * lax.rsqrt(jnp.mean(vectors * vectors, axis=-1, keepdims=True) + 1e-06)
    ).astype(jnp.bfloat16)


def pack_pairs(owners, embed, init_span, capacity, vert_count):
    row_count = embed.shape[0]
    target_dev = owners[:, 0]
    onehot = (target_dev[:, None] == jnp.arange(vert_count)[None, :]).astype(jnp.int32)
    before = jnp.cumsum(onehot, axis=0) - onehot
    place = jnp.sum(before * onehot, axis=1)
    lookup = (
        jnp.full((vert_count * capacity,), row_count, jnp.int32)
        .at[target_dev * capacity + place]
        .set(jnp.arange(row_count, dtype=jnp.int32))
    )
    blank = jnp.zeros((1, embed.shape[1]), jnp.bfloat16)
    padded_embed = jnp.concatenate([embed, blank], axis=0)
    padded_init = jnp.concatenate([init_span, blank], axis=0)
    anchors = padded_embed[lookup].reshape(vert_count, capacity, -1)
    keys_all = padded_init[lookup].reshape(vert_count, capacity, -1)
    flags = (lookup < row_count).astype(jnp.bfloat16).reshape(vert_count, capacity)
    return (anchors, keys_all, flags)


def score_pairs(anchors, keys_all, flags):
    feature_columns = anchors.shape[-1]
    query_rows = rms_rows(anchors.reshape(-1, feature_columns))
    normalized_keys = rms_rows(keys_all.reshape(-1, feature_columns))
    similarity_scores = jnp.dot(
        query_rows, normalized_keys.T, preferred_element_type=jnp.float32
    ) / (feature_columns * SOFTMAX_TEMP)
    live_mask = flags.reshape(-1).astype(jnp.float32)
    totals = jnp.sum(jnp.exp(similarity_scores) * live_mask[None, :], axis=1)
    diagonal = jnp.diagonal(similarity_scores)
    return (jnp.log(totals + 1.0 - live_mask) - diagonal) * live_mask


def local_by_section(
    init_feats,
    layer_weight,
    tile_cols,
    tile_vals,
    send_rows,
    send_count,
    recv_rows,
    recv_weight,
    pair_owner,
):
    segment_count = lax.axis_size("segment")
    vert_count = lax.axis_size("vert")
    position = lax.axis_index("segment")
    span_count, row_count, feature_columns = init_feats.shape
    capacity = 3 * row_count // (2 * vert_count)
    tile_size = tile_vals.shape[-1]
    tile_rows = row_count // tile_size
    slot_count = send_rows.shape[-1]
    weight = layer_weight[0]
    mixing = jnp.log(LAMBDA_DECAY / (position.astype(jnp.float32) + 1.0) + 1.0)
    row_ids = jnp.arange(row_count, dtype=jnp.int32)

    def section(span_id, hidden, init_span):
        columns = tile_cols[span_id]
        values = tile_vals[span_id]
        picked = hidden.reshape(tile_rows, tile_size, feature_columns)[columns]
        local_sum = jnp.einsum(
            "tij,tjd->tid", values, picked, preferred_element_type=jnp.float32
        ).reshape(row_count, feature_columns)
        retain = jnp.arange(slot_count)[None, :] < send_count[span_id][:, None]
        outgoing = jnp.where(
            retain[..., None], hidden[send_rows[span_id]], jnp.zeros((), jnp.bfloat16)
        )
        incoming = lax.all_to_all(outgoing, "vert", split_axis=0, concat_axis=0, tiled=True)
        targets = recv_rows[span_id].reshape(-1)
        edge_weights = recv_weight[span_id].reshape(-1)
        placing = jnp.where(
            targets[None, :] == row_ids[:, None], edge_weights[None, :], jnp.zeros((), jnp.bfloat16)
        )
        border = jnp.dot(
            placing, incoming.reshape(-1, feature_columns), preferred_element_type=jnp.float32
        )
        mixed = (1.0 - ALPHA_MIX) * (local_sum + border) + ALPHA_MIX * init_span.astype(jnp.float32)
        support = mixed.astype(jnp.bfloat16)
        product = jnp.dot(support, weight, preferred_element_type=jnp.float32)
        return jax.nn.relu((1.0 - mixing) * support.astype(jnp.float32) + mixing * product).astype(
            jnp.bfloat16
        )

    stored = jnp.zeros((span_count, row_count, feature_columns), jnp.bfloat16)

    def advance(moment, carry):
        arrived, stored_now = carry
        span_raw = moment - position
        active = (span_raw >= 0) & (span_raw < span_count)
        span_id = jnp.clip(span_raw, 0, span_count - 1)
        init_span = init_feats[span_id]
        hidden = jnp.where(position == 0, init_span, arrived)
        result = section(span_id, hidden, init_span)
        passed = from_behind(result, "segment", 1)
        stored_now = jnp.where(active, stored_now.at[span_id].set(result), stored_now)
        return (passed, stored_now)

    start_carry = (jnp.zeros((row_count, feature_columns), jnp.bfloat16), stored)
    final_carry = lax.fori_loop(0, span_count + segment_count - 1, advance, start_carry)
    stored = final_carry[1]

    def pack_one(owners, embed, init_span):
        return pack_pairs(owners, embed, init_span, capacity, vert_count)

    anchors, keys_all, flags = jax.vmap(pack_one)(pair_owner, stored, init_feats)
    got_anchors, got_keys, got_flags = (
        lax.all_to_all(anchors, "vert", split_axis=1, concat_axis=1, tiled=True),
        lax.all_to_all(keys_all, "vert", split_axis=1, concat_axis=1, tiled=True),
        lax.all_to_all(flags, "vert", split_axis=1, concat_axis=1, tiled=True),
    )
    losses = jax.vmap(score_pairs)(got_anchors, got_keys, got_flags)
    return losses[None]


def solution(mesh):
    specs = (
        P(None, "vert", None),
        P("segment", None, None),
        P(None, "vert"),
        P(None, "vert", None, None),
        P(None, "vert", None),
        P(None, "vert"),
        P(None, "vert", None),
        P(None, "vert", None),
        P(None, "vert", None),
    )
    out_spec = P("segment", None, "vert")
    if (mesh.shape["segment"], mesh.shape["vert"]) != (SEGMENTS, VERTS):
        return jax.shard_map(
            local_by_section, mesh=mesh, in_specs=specs, out_specs=out_spec, check_vma=False
        )
    parts = {"segment": AXES[:2], "vert": AXES[2:], None: None}
    fine = Mesh(mesh.devices.reshape((2,) * len(AXES)), AXES)

    def split(spec):
        return P(*[parts[name] for name in spec])

    return jax.shard_map(
        local,
        mesh=fine,
        in_specs=tuple(split(spec) for spec in specs),
        out_specs=split(out_spec),
        check_vma=False,
    )
```

```python
import functools
import itertools

import jax
import jax.numpy as jnp
import numpy as np
from jax import lax
from jax.experimental import pallas as pl
from jax.experimental.pallas import tpu as pltpu
from jax.sharding import Mesh
from jax.sharding import PartitionSpec as P

ALPHA_MIX = 0.5
LAMBDA_DECAY = 0.5
SOFTMAX_TEMP = 0.1
NORM_EPS = 1e-06

AXES = ("x", "core", "zh", "zl", "y")
SPANS, SEGMENTS, VERTS = 4, 4, 8
SMALL_ROWS = 16
LANES = 128
SEND, RECV, WEIGHT, COLS, OWNER = 0, 128, 256, 512, 640


ARRIVALS = {1: (0, 0), 2: (0, 1), 4: (0, 2), 3: (1, 0), 5: (1, 1), 6: (2, 0), 7: (3, 0)}


def exchange(block, *across, core=None):
    sizes = [range(lax.axis_size(name)) for name in AXES]
    pairs = []
    for index, here in enumerate(itertools.product(*sizes)):
        there = [1 - at if name in across else at for name, at in zip(AXES, here, strict=True)]
        target = functools.reduce(lambda total, digit: total * 2 + digit, there, 0)
        if core is None or here[1] == core:
            pairs.append((index, target))
    return lax.ppermute(block, AXES, pairs)


def rms_unit(vectors):
    scale = lax.rsqrt(jnp.mean(vectors * vectors, axis=-1, keepdims=True) + NORM_EPS)
    return (vectors * scale).astype(jnp.bfloat16)


def mixing_of(layer):
    return float(np.log(np.float32(LAMBDA_DECAY) / np.float32(layer + 1) + np.float32(1.0)))


def turned(matrix):
    rows, columns = matrix.shape
    whole = jnp.concatenate([matrix, jnp.zeros((rows, LANES - columns), matrix.dtype)], axis=1)
    return jnp.transpose(whole)[:columns]


def pack_kernel(
    init_ref, tiles_ref, send_ref, count_ref, recv_ref, weight_ref, cols_ref, owner_ref,
    mine_ref, other_ref, small, sems,
):
    x, core, zh = [lax.axis_index(name) for name in AXES[:3]]
    half, width = mine_ref.shape[0] - SMALL_ROWS, init_ref.shape[-1]
    peers, slots = send_ref.shape[1:]
    tiles, rows = cols_ref.shape[0], owner_ref.shape[-1]
    lane = lax.broadcasted_iota(jnp.int32, (1, LANES), 1)
    first = pl.multiple_of(core * half, half)
    spans = (zh * 2 + x, (1 - zh) * 2 + x)
    copies = []
    for i, out_ref in enumerate((mine_ref, other_ref)):
        copies.append(
            pltpu.make_async_copy(
                init_ref.at[spans[i], pl.ds(first, half), :],
                out_ref.at[pl.ds(0, half), pl.ds(0, width)],
                sems.at[2 * i],
            )
        )
        copies.append(
            pltpu.make_async_copy(
                tiles_ref.at[spans[i], core],
                out_ref.at[pl.ds(0, half), pl.ds(width, half)],
                sems.at[2 * i + 1],
            )
        )
    for copy in copies:
        copy.start()
    small[...] = jnp.zeros_like(small)
    for i, out_ref in enumerate((mine_ref, other_ref)):
        span = spans[i]
        sends = turned(send_ref[span].astype(jnp.float32))
        used = lax.broadcasted_iota(jnp.int32, (slots, peers), 0) < count_ref[pl.ds(span, 1), :]
        small[i, 0:slots, SEND : SEND + peers] = jnp.where(used, sends, float(rows))
        small[i, 0:slots, RECV : RECV + peers] = turned(recv_ref[span].astype(jnp.float32))
        small[i, 0:slots, WEIGHT : WEIGHT + peers] = turned(weight_ref[span].astype(jnp.float32))
        columns = jnp.zeros((1, LANES), jnp.int32)
        for t in range(tiles):
            columns = jnp.where(lane == t, cols_ref[t, span], columns)
        small[i, 0:1, COLS : COLS + LANES] = columns.astype(jnp.float32)
        small[i, 0:1, OWNER : OWNER + rows] = owner_ref[span].astype(jnp.float32)
        out_ref[half : half + SMALL_ROWS, :] = small[i].astype(jnp.bfloat16)
    for copy in copies:
        copy.wait()


def support_of(block, spread_ref, cols_ref, init_ref, hidden, boundary):
    tile = spread_ref.shape[1]
    rows = init_ref.shape[1]
    incoming = boundary[block].astype(jnp.bfloat16)
    depth = tile + incoming.shape[0]
    parts = []
    for t in range(rows // tile):
        column = cols_ref[block, t]
        start = pl.multiple_of(column * tile, tile)
        source = jnp.concatenate([hidden[block, pl.ds(start, tile), :], incoming], axis=0)
        gathered = jnp.dot(
            spread_ref[block * (rows // tile) + t, :, 0:depth],
            source,
            preferred_element_type=jnp.float32,
        )
        init = init_ref[block, t * tile : (t + 1) * tile, :].astype(jnp.float32)
        parts.append(((1.0 - ALPHA_MIX) * gathered + ALPHA_MIX * init).astype(jnp.bfloat16))
    return jnp.concatenate(parts, axis=0)


def transform(support, weight, mixing):
    product = jnp.dot(support, weight, preferred_element_type=jnp.float32)
    blended = (1.0 - mixing) * support.astype(jnp.float32) + mixing * product
    return jnp.maximum(blended, 0.0).astype(jnp.bfloat16)


def publish(block, block_out, pick_ref, boundary, target):
    receivers, border, _ = boundary.shape
    each = border // receivers
    picked = jnp.dot(pick_ref[block], block_out, preferred_element_type=jnp.float32)
    border_start = pl.multiple_of(block * each, each)
    for receiver in range(receivers):
        boundary[receiver, pl.ds(border_start, each), :] = picked[
            receiver * each : (receiver + 1) * each
        ]
    slots = target.shape[0] // receivers
    slot_start = pl.multiple_of(block * slots, slots)
    target[pl.ds(slot_start, slots), :] = rms_unit(picked[border:])


def score(keys, anchors, live_ref):
    total, width = keys.shape
    logits = lax.dot_general(
        keys[...], anchors[...], (((1,), (1,)), ((), ())), preferred_element_type=jnp.float32
    ) / (width * SOFTMAX_TEMP)
    live = live_ref[:, 0:1]
    key_ids = lax.broadcasted_iota(jnp.int32, (total, total), 0)
    anchor_ids = lax.broadcasted_iota(jnp.int32, (total, total), 1)
    same = key_ids == anchor_ids
    live_row = jnp.sum(jnp.where(same, live, 0.0), axis=0, keepdims=True)
    totals = jnp.sum(jnp.exp(logits) * live, axis=0, keepdims=True)
    diagonal = jnp.sum(jnp.where(same, logits, 0.0), axis=0, keepdims=True)
    return (jnp.log(totals + 1.0 - live_row) - diagonal) * live_row


def run_layer(spread_ref, cols_ref, init_ref, pick_ref, source, border_in, weight, mixing,
              target, border_out, anchors, group=2, unroll=4):
    blocks, rows, _ = init_ref.shape

    def advance(chunk, carry):
        support = jnp.concatenate(
            [
                support_of(chunk * group + k, spread_ref, cols_ref, init_ref, source, border_in)
                for k in range(group)
            ],
            axis=0,
        )
        out = transform(support, weight[...], mixing)
        for k in range(group):
            block_out = out[k * rows : (k + 1) * rows]
            target[chunk * group + k] = block_out
            publish(chunk * group + k, block_out, pick_ref, border_out, anchors)
        return carry

    lax.fori_loop(0, blocks // group, advance, 0, unroll=unroll)


def first_kernel(
    init_feats, tile_vals, mine_ref, *rest
):
    blocks = VERTS
    nets, flips, weights = rest[:4], rest[4:8], rest[8:12]
    (init_ref, spread_ref, pick_ref, cols_out, live_ref, keys, hidden, boundary, loss_ref,
     boundary0, anchors, small, weight, cols_ref, sems, weight_sems) = rest[12:]
    x, core, zh, zl, y = [lax.axis_index(name) for name in AXES]
    vert = zh * 4 + zl * 2 + y
    rows, width = init_ref.shape[1:]
    half = rows // 2
    tile = spread_ref.shape[1]
    tiles = rows // tile
    border = boundary.shape[1]
    each = border // blocks
    slots = keys.shape[0] // blocks

    def start(source, target, sem):
        copy = pltpu.make_async_copy(source, target, sem)
        copy.start()
        return copy

    for place, source in enumerate(weights):
        by_x, by_core = place // 2, place % 2

        @pl.when((x == by_x) & (core == by_core))
        def _():
            pltpu.make_async_copy(source, weight, weight_sems.at[0]).start()

    span = zh * 2 + x
    copies = [
        start(init_feats.at[span], init_ref.at[vert], sems.at[0]),
        start(mine_ref.at[pl.ds(half, SMALL_ROWS), :], small.at[vert], sems.at[1]),
    ]
    at = 2
    for t in range(tiles):
        target = spread_ref.at[vert * tiles + t, :, pl.ds(0, tile)]
        copies.append(start(tile_vals.at[span, t], target, sems.at[at]))
        at += 1
    for k in range(1, blocks):
        block = vert ^ k
        group, index = ARRIVALS[k]
        base = index * (half + SMALL_ROWS)
        for part, source in ((core, nets[group]), (1 - core, flips[group])):
            first = pl.multiple_of(part * half, half)
            copies.append(
                start(
                    source.at[pl.ds(base, half), pl.ds(0, width)],
                    init_ref.at[block, pl.ds(first, half), :],
                    sems.at[at],
                )
            )
            copies.append(
                start(
                    source.at[pl.ds(base, half), pl.ds(width, tile)],
                    spread_ref.at[block * tiles + part, :, pl.ds(0, tile)],
                    sems.at[at + 1],
                )
            )
            at += 2
        source = nets[group].at[pl.ds(base + half, SMALL_ROWS), :]
        copies.append(start(source, small.at[block], sems.at[at]))
        at += 1
    for copy in copies:
        copy.wait()

    owner = core * 4 + zl * 2 + y
    tables = [small[block].astype(jnp.float32) for block in range(blocks)]
    owners = jnp.concatenate([table[0:1, OWNER : OWNER + rows] for table in tables], axis=0)
    cols_out[...] = jnp.concatenate(
        [table[0:1, COLS : COLS + LANES] for table in tables], axis=0
    ).astype(jnp.int32)
    to_scalar = start(cols_out, cols_ref, sems.at[at])
    owned = jnp.where(owners == owner.astype(jnp.float32), 1.0, 0.0)
    earlier = lax.broadcasted_iota(jnp.int32, (rows, rows), 0) < lax.broadcasted_iota(
        jnp.int32, (rows, rows), 1
    )
    rank = jnp.dot(
        owned.astype(jnp.bfloat16),
        jnp.where(earlier, 1.0, 0.0).astype(jnp.bfloat16),
        preferred_element_type=jnp.float32,
    )
    row_ids = lax.broadcasted_iota(jnp.int32, (each, rows), 1).astype(jnp.float32)
    slot_ids = lax.broadcasted_iota(jnp.int32, (slots, rows), 0).astype(jnp.float32)
    for block in range(blocks):
        table = tables[block]
        sends = [
            jnp.where(table[0:each, SEND + peer : SEND + peer + 1] == row_ids, 1.0, 0.0)
            for peer in range(blocks)
        ]
        fills = jnp.where(
            slot_ids == rank[block : block + 1], owned[block : block + 1], 0.0
        )
        pick_ref[block] = jnp.concatenate(sends + [fills], axis=0).astype(jnp.bfloat16)
        live_ref[block * slots : (block + 1) * slots, :] = jnp.broadcast_to(
            jnp.sum(fills, axis=1, keepdims=True), (slots, LANES)
        )
        placing = [
            jnp.where(
                table[0:each, RECV + peer : RECV + peer + 1] == row_ids,
                table[0:each, WEIGHT + peer : WEIGHT + peer + 1],
                0.0,
            )
            for peer in range(blocks)
        ]
        placing = jnp.concatenate(
            placing + [jnp.zeros((LANES - border, rows), jnp.float32)], axis=0
        )
        placing = jnp.transpose(placing).astype(jnp.bfloat16)
        for t in range(tiles):
            spread_ref[block * tiles + t, :, tile : tile + LANES] = placing[
                t * tile : (t + 1) * tile
            ]

    def begin(block, carry):
        publish(block, init_ref[block], pick_ref, boundary0, keys)
        return carry

    lax.fori_loop(0, blocks, begin, 0, unroll=4)
    to_scalar.wait()
    pltpu.make_async_copy(weights[0], weight, weight_sems.at[0]).wait()
    run_layer(
        spread_ref, cols_ref, init_ref, pick_ref, init_ref, boundary0, weight, mixing_of(0),
        hidden, boundary, anchors,
    )
    loss_ref[...] = score(keys, anchors, live_ref)


def rest_kernel(
    cols_ref, init_ref, spread_ref, pick_ref, live_ref, keys, hidden, boundary,
    loss0_ref, own_ref, flip_ref, even_ref, even_flip_ref, odd_ref, odd_other_ref,
    odd_flip_ref, odd_other_flip_ref, loss_ref, held, border_held, anchors, last, weight,
    weight_sems,
):
    x, core, zl = [lax.axis_index(name) for name in ("x", "core", "zl")]
    layers = SEGMENTS
    blocks = init_ref.shape[0]
    slots = keys.shape[0] // blocks
    half = weight.shape[1] // 2

    def fetch(layer):
        slot, by_x, by_core = layer % 2, layer // 2, layer % 2

        def load(source, part, to):
            first = part * half if isinstance(part, int) else pl.multiple_of(part * half, half)
            pltpu.make_async_copy(
                source, weight.at[slot, pl.ds(first, half), :], weight_sems.at[slot, to]
            ).start()

        def load_whole(source):
            for part in range(2):
                load(source.at[pl.ds(part * half, half), :], part, part)

        near = x == by_x
        pl.when(near & (core == by_core))(lambda: load_whole(own_ref))
        pl.when(near & (core != by_core))(lambda: load_whole(flip_ref))
        if by_core == 0:
            pl.when((x != by_x) & (core == 0))(lambda: load_whole(even_ref))
            pl.when((x != by_x) & (core == 1))(lambda: load_whole(even_flip_ref))
        else:

            @pl.when((x != by_x) & (core == 1))
            def _():
                load(odd_ref, zl, 0)
                load(odd_other_ref, 1 - zl, 1)

            @pl.when((x != by_x) & (core == 0))
            def _():
                load(odd_flip_ref, zl, 0)
                load(odd_other_flip_ref, 1 - zl, 1)

    def arrive(layer):
        slot = layer % 2
        for part in range(2):
            pltpu.make_async_copy(
                own_ref.at[pl.ds(part * half, half), :],
                weight.at[slot, pl.ds(part * half, half), :],
                weight_sems.at[slot, part],
            ).wait()

    fetch(1)

    def report(layer, losses):
        for copy in range(2):
            loss_ref[2 * layer + copy] = losses

    report(0, loss0_ref[...])
    source, border_in = hidden, boundary
    for layer in range(1, layers - 1):
        arrive(layer)
        fetch(layer + 1)
        target, border_out = held.at[layer % 2], border_held.at[layer % 2]
        run_layer(
            spread_ref, cols_ref, init_ref, pick_ref, source, border_in, weight.at[layer % 2],
            mixing_of(layer), target, border_out, anchors,
        )
        report(layer, score(keys, anchors, live_ref))
        source, border_in = target, border_out

    border = boundary.shape[1]

    def choose(block, carry):
        support = support_of(block, spread_ref, cols_ref, init_ref, source, border_in)
        chosen = jnp.dot(pick_ref[block, border:, :], support, preferred_element_type=jnp.float32)
        slot_start = pl.multiple_of(block * slots, slots)
        last[pl.ds(slot_start, slots), :] = chosen.astype(jnp.bfloat16)
        return carry

    lax.fori_loop(0, blocks, choose, 0, unroll=4)
    arrive(layers - 1)
    final = transform(last[...], weight[(layers - 1) % 2], mixing_of(layers - 1))
    anchors[...] = rms_unit(final.astype(jnp.float32))
    report(layers - 1, score(keys, anchors, live_ref))


VMEM = pl.BlockSpec(memory_space=pltpu.VMEM)
SMEM = pl.BlockSpec(memory_space=pltpu.SMEM)
HBM = pl.BlockSpec(memory_space=pltpu.HBM)
FIRST_VMEM = 20 * 1024 * 1024
REST_VMEM = 26 * 1024 * 1024


def local(
    init_feats,
    layer_weight,
    tile_cols,
    tile_vals,
    send_rows,
    send_count,
    recv_rows,
    recv_weight,
    pair_owner,
):
    span_count, rows, width = init_feats.shape
    tile = tile_vals.shape[-1]
    tiles = rows // tile
    blocks = VERTS
    border = blocks * send_rows.shape[-1]
    slots = 3 * rows // (2 * blocks)
    total = blocks * slots
    half = rows // 2
    bf16, f32 = jnp.bfloat16, jnp.float32
    shape = jax.ShapeDtypeStruct
    zh, zl = lax.axis_index("zh"), lax.axis_index("zl")
    own = layer_weight[0]

    packed = shape((half + SMALL_ROWS, width + tile), bf16)
    mine, other = pl.pallas_call(
        pack_kernel,
        out_shape=(packed, packed),
        in_specs=[HBM, HBM] + [VMEM] * 4 + [SMEM, VMEM],
        out_specs=(VMEM, VMEM),
        scratch_shapes=[
            pltpu.VMEM((2, SMALL_ROWS, width + tile), f32),
            pltpu.SemaphoreType.DMA((4,)),
        ],
    )(
        init_feats, tile_vals, send_rows, send_count, recv_rows, recv_weight, tile_cols.T,
        jnp.swapaxes(pair_owner, 1, 2),
    )

    own, mine, other = lax.optimization_barrier((own, mine, other))
    net4, net2, net1 = exchange(other, "zh"), exchange(mine, "zl"), exchange(mine, "y")
    even = exchange(own, "x", core=0)
    odd_part = lax.dynamic_slice(own, (zl * (width // 2), 0), (width // 2, width))
    odd = exchange(odd_part, "x", core=1)
    net1, net2, net4 = lax.optimization_barrier((net1, net2, net4))
    net6 = exchange(net4, "zl")
    net35 = exchange(jnp.concatenate([net2, net4]), "y")
    net124 = jnp.concatenate([net1, net2, net4])
    flip124 = exchange(net124, "core")
    net7 = exchange(net6, "y")
    flip = exchange(own, "core")
    net35, flip124, net6, odd, even = lax.optimization_barrier((net35, flip124, net6, odd, even))
    flip35, flip6 = exchange(net35, "core"), exchange(net6, "core")
    even_flip = exchange(even, "core", core=0)
    odd_other = exchange(odd, "zl", core=1)
    net7, flip35, flip6, even_flip = lax.optimization_barrier((net7, flip35, flip6, even_flip))
    flip7 = exchange(net7, "core")

    keep = [
        shape((blocks, rows, width), bf16),
        shape((blocks * tiles, tile, tile + LANES), bf16),
        shape((blocks, border + slots, rows), bf16),
        shape((blocks, LANES), jnp.int32),
        shape((total, LANES), f32),
        shape((total, width), bf16),
        shape((blocks, rows, width), bf16),
        shape((blocks, border, width), f32),
        shape((1, total), f32),
    ]
    init, spread, pick, cols, live, keys, hidden, boundary, loss0 = pl.pallas_call(
        first_kernel,
        out_shape=keep,
        in_specs=[HBM] * 15,
        out_specs=[VMEM] * len(keep),
        scratch_shapes=[
            pltpu.VMEM((blocks, border, width), f32),
            pltpu.VMEM((total, width), bf16),
            pltpu.VMEM((blocks, SMALL_ROWS, width + tile), bf16),
            pltpu.VMEM((width, width), bf16),
            pltpu.SMEM((blocks, LANES), jnp.int32),
            pltpu.SemaphoreType.DMA((8 * blocks,)),
            pltpu.SemaphoreType.DMA((1,)),
        ],
        compiler_params=pltpu.CompilerParams(vmem_limit_bytes=FIRST_VMEM),
        cost_estimate=pl.CostEstimate(
            flops=2 * blocks * rows * width * width, bytes_accessed=1 << 24, transcendentals=0
        ),
    )(
        init_feats, tile_vals, mine, net124, net35, net6, net7, flip124, flip35, flip6, flip7,
        own, flip, even, even_flip,
    )
    odd, odd_other, loss0 = lax.optimization_barrier((odd, odd_other, loss0))
    odd_flip = exchange(odd, "core", core=1)
    odd_other_flip = exchange(odd_other, "core", core=1)
    losses = pl.pallas_call(
        rest_kernel,
        out_shape=shape((2 * SEGMENTS, 1, total), f32),
        in_specs=[SMEM] + [VMEM] * 8 + [HBM] * 8,
        out_specs=VMEM,
        scratch_shapes=[
            pltpu.VMEM((2, blocks, rows, width), bf16),
            pltpu.VMEM((2, blocks, border, width), f32),
            pltpu.VMEM((total, width), bf16),
            pltpu.VMEM((total, width), bf16),
            pltpu.VMEM((2, width, width), bf16),
            pltpu.SemaphoreType.DMA((2, 2)),
        ],
        compiler_params=pltpu.CompilerParams(vmem_limit_bytes=REST_VMEM),
        cost_estimate=pl.CostEstimate(
            flops=6 * blocks * rows * width * width, bytes_accessed=1 << 24, transcendentals=0
        ),
    )(
        cols, init, spread, pick, live, keys, hidden, boundary, loss0, own, flip, even,
        even_flip, odd, odd_other, odd_flip, odd_other_flip,
    )
    losses = lax.all_to_all(losses, ("x", "core", "zh"), split_axis=0, concat_axis=0, tiled=True)
    losses = lax.dynamic_index_in_dim(
        losses.reshape(2, 2, 2, total), zh, axis=1, keepdims=False
    )
    return jnp.swapaxes(losses, 0, 1).reshape(1, span_count, total)


def from_behind(block, axis, distance):
    devices = range(lax.axis_size(axis))
    route = [(i - distance, i) for i in devices if i - distance in devices]
    return lax.ppermute(block, axis, route)


def rms_rows(vectors):
    vectors = vectors.astype(jnp.float32)
    return (
        vectors * lax.rsqrt(jnp.mean(vectors * vectors, axis=-1, keepdims=True) + 1e-06)
    ).astype(jnp.bfloat16)


def pack_pairs(owners, embed, init_span, capacity, vert_count):
    row_count = embed.shape[0]
    target_dev = owners[:, 0]
    onehot = (target_dev[:, None] == jnp.arange(vert_count)[None, :]).astype(jnp.int32)
    before = jnp.cumsum(onehot, axis=0) - onehot
    place = jnp.sum(before * onehot, axis=1)
    lookup = (
        jnp.full((vert_count * capacity,), row_count, jnp.int32)
        .at[target_dev * capacity + place]
        .set(jnp.arange(row_count, dtype=jnp.int32))
    )
    blank = jnp.zeros((1, embed.shape[1]), jnp.bfloat16)
    padded_embed = jnp.concatenate([embed, blank], axis=0)
    padded_init = jnp.concatenate([init_span, blank], axis=0)
    anchors = padded_embed[lookup].reshape(vert_count, capacity, -1)
    keys_all = padded_init[lookup].reshape(vert_count, capacity, -1)
    flags = (lookup < row_count).astype(jnp.bfloat16).reshape(vert_count, capacity)
    return (anchors, keys_all, flags)


def score_pairs(anchors, keys_all, flags):
    feature_columns = anchors.shape[-1]
    query_rows = rms_rows(anchors.reshape(-1, feature_columns))
    normalized_keys = rms_rows(keys_all.reshape(-1, feature_columns))
    similarity_scores = jnp.dot(
        query_rows, normalized_keys.T, preferred_element_type=jnp.float32
    ) / (feature_columns * SOFTMAX_TEMP)
    live_mask = flags.reshape(-1).astype(jnp.float32)
    totals = jnp.sum(jnp.exp(similarity_scores) * live_mask[None, :], axis=1)
    diagonal = jnp.diagonal(similarity_scores)
    return (jnp.log(totals + 1.0 - live_mask) - diagonal) * live_mask


def local_by_section(
    init_feats,
    layer_weight,
    tile_cols,
    tile_vals,
    send_rows,
    send_count,
    recv_rows,
    recv_weight,
    pair_owner,
):
    segment_count = lax.axis_size("segment")
    vert_count = lax.axis_size("vert")
    position = lax.axis_index("segment")
    span_count, row_count, feature_columns = init_feats.shape
    capacity = 3 * row_count // (2 * vert_count)
    tile_size = tile_vals.shape[-1]
    tile_rows = row_count // tile_size
    slot_count = send_rows.shape[-1]
    weight = layer_weight[0]
    mixing = jnp.log(LAMBDA_DECAY / (position.astype(jnp.float32) + 1.0) + 1.0)
    row_ids = jnp.arange(row_count, dtype=jnp.int32)

    def section(span_id, hidden, init_span):
        columns = tile_cols[span_id]
        values = tile_vals[span_id]
        picked = hidden.reshape(tile_rows, tile_size, feature_columns)[columns]
        local_sum = jnp.einsum(
            "tij,tjd->tid", values, picked, preferred_element_type=jnp.float32
        ).reshape(row_count, feature_columns)
        retain = jnp.arange(slot_count)[None, :] < send_count[span_id][:, None]
        outgoing = jnp.where(
            retain[..., None], hidden[send_rows[span_id]], jnp.zeros((), jnp.bfloat16)
        )
        incoming = lax.all_to_all(outgoing, "vert", split_axis=0, concat_axis=0, tiled=True)
        targets = recv_rows[span_id].reshape(-1)
        edge_weights = recv_weight[span_id].reshape(-1)
        placing = jnp.where(
            targets[None, :] == row_ids[:, None], edge_weights[None, :], jnp.zeros((), jnp.bfloat16)
        )
        border = jnp.dot(
            placing, incoming.reshape(-1, feature_columns), preferred_element_type=jnp.float32
        )
        mixed = (1.0 - ALPHA_MIX) * (local_sum + border) + ALPHA_MIX * init_span.astype(jnp.float32)
        support = mixed.astype(jnp.bfloat16)
        product = jnp.dot(support, weight, preferred_element_type=jnp.float32)
        return jax.nn.relu((1.0 - mixing) * support.astype(jnp.float32) + mixing * product).astype(
            jnp.bfloat16
        )

    stored = jnp.zeros((span_count, row_count, feature_columns), jnp.bfloat16)

    def advance(moment, carry):
        arrived, stored_now = carry
        span_raw = moment - position
        active = (span_raw >= 0) & (span_raw < span_count)
        span_id = jnp.clip(span_raw, 0, span_count - 1)
        init_span = init_feats[span_id]
        hidden = jnp.where(position == 0, init_span, arrived)
        result = section(span_id, hidden, init_span)
        passed = from_behind(result, "segment", 1)
        stored_now = jnp.where(active, stored_now.at[span_id].set(result), stored_now)
        return (passed, stored_now)

    start_carry = (jnp.zeros((row_count, feature_columns), jnp.bfloat16), stored)
    final_carry = lax.fori_loop(0, span_count + segment_count - 1, advance, start_carry)
    stored = final_carry[1]

    def pack_one(owners, embed, init_span):
        return pack_pairs(owners, embed, init_span, capacity, vert_count)

    anchors, keys_all, flags = jax.vmap(pack_one)(pair_owner, stored, init_feats)
    got_anchors, got_keys, got_flags = (
        lax.all_to_all(anchors, "vert", split_axis=1, concat_axis=1, tiled=True),
        lax.all_to_all(keys_all, "vert", split_axis=1, concat_axis=1, tiled=True),
        lax.all_to_all(flags, "vert", split_axis=1, concat_axis=1, tiled=True),
    )
    losses = jax.vmap(score_pairs)(got_anchors, got_keys, got_flags)
    return losses[None]


def solution(mesh):
    specs = (
        P(None, "vert", None),
        P("segment", None, None),
        P(None, "vert"),
        P(None, "vert", None, None),
        P(None, "vert", None),
        P(None, "vert"),
        P(None, "vert", None),
        P(None, "vert", None),
        P(None, "vert", None),
    )
    out_spec = P("segment", None, "vert")
    if (mesh.shape["segment"], mesh.shape["vert"]) != (SEGMENTS, VERTS):
        return jax.shard_map(
            local_by_section, mesh=mesh, in_specs=specs, out_specs=out_spec, check_vma=False
        )
    parts = {"segment": AXES[:2], "vert": AXES[2:], None: None}
    fine = Mesh(mesh.devices.reshape((2,) * len(AXES)), AXES)

    def split(spec):
        return P(*[parts[name] for name in spec])

    return jax.shard_map(
        local,
        mesh=fine,
        in_specs=tuple(split(spec) for spec in specs),
        out_specs=split(out_spec),
        check_vma=False,
    )
```

```python
import functools
import itertools

import jax
import jax.numpy as jnp
import numpy as np
from jax import lax
from jax.experimental import pallas as pl
from jax.experimental.pallas import tpu as pltpu
from jax.sharding import Mesh
from jax.sharding import PartitionSpec as P

ALPHA_MIX = 0.5
LAMBDA_DECAY = 0.5
SOFTMAX_TEMP = 0.1
NORM_EPS = 1e-06

AXES = ("x", "core", "zh", "zl", "y")
SPANS, SEGMENTS, VERTS = 4, 4, 8
SMALL_ROWS = 16
LANES = 128
SEND, RECV, WEIGHT, COLS, OWNER = 0, 128, 256, 512, 640


ARRIVALS = {1: (0, 0), 2: (0, 1), 4: (0, 2), 3: (1, 0), 5: (1, 1), 6: (2, 0), 7: (3, 0)}


def exchange(block, *across, core=None):
    sizes = [range(lax.axis_size(name)) for name in AXES]
    pairs = []
    for index, here in enumerate(itertools.product(*sizes)):
        there = [1 - at if name in across else at for name, at in zip(AXES, here, strict=True)]
        target = functools.reduce(lambda total, digit: total * 2 + digit, there, 0)
        if core is None or here[1] == core:
            pairs.append((index, target))
    return lax.ppermute(block, AXES, pairs)


def rms_unit(vectors):
    scale = lax.rsqrt(jnp.mean(vectors * vectors, axis=-1, keepdims=True) + NORM_EPS)
    return (vectors * scale).astype(jnp.bfloat16)


def mixing_of(layer):
    return float(np.log(np.float32(LAMBDA_DECAY) / np.float32(layer + 1) + np.float32(1.0)))


def turned(matrix):
    rows, columns = matrix.shape
    whole = jnp.concatenate([matrix, jnp.zeros((rows, LANES - columns), matrix.dtype)], axis=1)
    return jnp.transpose(whole)[:columns]


def pack_kernel(
    init_ref, tiles_ref, send_ref, count_ref, recv_ref, weight_ref, cols_ref, owner_ref,
    mine_ref, other_ref, small, sems,
):
    x, core, zh = [lax.axis_index(name) for name in AXES[:3]]
    half, width = mine_ref.shape[0] - SMALL_ROWS, init_ref.shape[-1]
    peers, slots = send_ref.shape[1:]
    tiles, rows = cols_ref.shape[0], owner_ref.shape[-1]
    lane = lax.broadcasted_iota(jnp.int32, (1, LANES), 1)
    first = pl.multiple_of(core * half, half)
    spans = (zh * 2 + x, (1 - zh) * 2 + x)
    copies = []
    for i, out_ref in enumerate((mine_ref, other_ref)):
        copies.append(
            pltpu.make_async_copy(
                init_ref.at[spans[i], pl.ds(first, half), :],
                out_ref.at[pl.ds(0, half), pl.ds(0, width)],
                sems.at[2 * i],
            )
        )
        copies.append(
            pltpu.make_async_copy(
                tiles_ref.at[spans[i], core],
                out_ref.at[pl.ds(0, half), pl.ds(width, half)],
                sems.at[2 * i + 1],
            )
        )
    for copy in copies:
        copy.start()
    small[...] = jnp.zeros_like(small)
    for i, out_ref in enumerate((mine_ref, other_ref)):
        span = spans[i]
        sends = turned(send_ref[span].astype(jnp.float32))
        used = lax.broadcasted_iota(jnp.int32, (slots, peers), 0) < count_ref[pl.ds(span, 1), :]
        small[i, 0:slots, SEND : SEND + peers] = jnp.where(used, sends, float(rows))
        small[i, 0:slots, RECV : RECV + peers] = turned(recv_ref[span].astype(jnp.float32))
        small[i, 0:slots, WEIGHT : WEIGHT + peers] = turned(weight_ref[span].astype(jnp.float32))
        columns = jnp.zeros((1, LANES), jnp.int32)
        for t in range(tiles):
            columns = jnp.where(lane == t, cols_ref[t, span], columns)
        small[i, 0:1, COLS : COLS + LANES] = columns.astype(jnp.float32)
        small[i, 0:1, OWNER : OWNER + rows] = owner_ref[span].astype(jnp.float32)
        out_ref[half : half + SMALL_ROWS, :] = small[i].astype(jnp.bfloat16)
    for copy in copies:
        copy.wait()


def support_of(block, spread_ref, cols_ref, init_ref, hidden, boundary):
    tile = spread_ref.shape[1]
    rows = init_ref.shape[1]
    incoming = boundary[block].astype(jnp.bfloat16)
    depth = tile + incoming.shape[0]
    parts = []
    for t in range(rows // tile):
        column = cols_ref[block, t]
        start = pl.multiple_of(column * tile, tile)
        source = jnp.concatenate([hidden[block, pl.ds(start, tile), :], incoming], axis=0)
        gathered = jnp.dot(
            spread_ref[block * (rows // tile) + t, :, 0:depth],
            source,
            preferred_element_type=jnp.float32,
        )
        init = init_ref[block, t * tile : (t + 1) * tile, :].astype(jnp.float32)
        parts.append(((1.0 - ALPHA_MIX) * gathered + ALPHA_MIX * init).astype(jnp.bfloat16))
    return jnp.concatenate(parts, axis=0)


def transform(support, weight, mixing):
    product = jnp.dot(support, weight, preferred_element_type=jnp.float32)
    blended = (1.0 - mixing) * support.astype(jnp.float32) + mixing * product
    return jnp.maximum(blended, 0.0).astype(jnp.bfloat16)


def publish(block, block_out, pick_ref, boundary, target):
    receivers, border, _ = boundary.shape
    each = border // receivers
    picked = jnp.dot(pick_ref[block], block_out, preferred_element_type=jnp.float32)
    border_start = pl.multiple_of(block * each, each)
    for receiver in range(receivers):
        boundary[receiver, pl.ds(border_start, each), :] = picked[
            receiver * each : (receiver + 1) * each
        ]
    slots = target.shape[0] // receivers
    slot_start = pl.multiple_of(block * slots, slots)
    target[pl.ds(slot_start, slots), :] = rms_unit(picked[border:])


def score(keys, anchors, live_ref):
    total, width = keys.shape
    logits = lax.dot_general(
        keys[...], anchors[...], (((1,), (1,)), ((), ())), preferred_element_type=jnp.float32
    ) / (width * SOFTMAX_TEMP)
    live = live_ref[:, 0:1]
    key_ids = lax.broadcasted_iota(jnp.int32, (total, total), 0)
    anchor_ids = lax.broadcasted_iota(jnp.int32, (total, total), 1)
    same = key_ids == anchor_ids
    live_row = jnp.sum(jnp.where(same, live, 0.0), axis=0, keepdims=True)
    totals = jnp.sum(jnp.exp(logits) * live, axis=0, keepdims=True)
    diagonal = jnp.sum(jnp.where(same, logits, 0.0), axis=0, keepdims=True)
    return (jnp.log(totals + 1.0 - live_row) - diagonal) * live_row


def run_layer(spread_ref, cols_ref, init_ref, pick_ref, source, border_in, weight, mixing,
              target, border_out, anchors, meanwhile, group=2):
    blocks, rows, _ = init_ref.shape
    for first in range(0, blocks, group):
        support = jnp.concatenate(
            [
                support_of(first + k, spread_ref, cols_ref, init_ref, source, border_in)
                for k in range(group)
            ],
            axis=0,
        )
        if first == 0:
            meanwhile()
        out = transform(support, weight[...], mixing)
        for k in range(group):
            block_out = out[k * rows : (k + 1) * rows]
            target[first + k] = block_out
            publish(first + k, block_out, pick_ref, border_out, anchors)


def first_kernel(
    init_feats, tile_vals, mine_ref, *rest
):
    blocks = VERTS
    nets, flips, weights = rest[:4], rest[4:8], rest[8:12]
    (init_ref, spread_ref, pick_ref, cols_out, live_ref, keys, hidden, boundary, loss_ref,
     boundary0, anchors, small, weight, cols_ref, sems, weight_sems) = rest[12:]
    x, core, zh, zl, y = [lax.axis_index(name) for name in AXES]
    vert = zh * 4 + zl * 2 + y
    rows, width = init_ref.shape[1:]
    half = rows // 2
    tile = spread_ref.shape[1]
    tiles = rows // tile
    border = boundary.shape[1]
    each = border // blocks
    slots = keys.shape[0] // blocks

    def start(source, target, sem):
        copy = pltpu.make_async_copy(source, target, sem)
        copy.start()
        return copy

    for place, source in enumerate(weights):
        by_x, by_core = place // 2, place % 2

        @pl.when((x == by_x) & (core == by_core))
        def _():
            pltpu.make_async_copy(source, weight, weight_sems.at[0]).start()

    span = zh * 2 + x
    tables = [start(mine_ref.at[pl.ds(half, SMALL_ROWS), :], small.at[vert], sems.at[0])]
    at = 1
    for k in range(1, blocks):
        group, index = ARRIVALS[k]
        source = nets[group].at[pl.ds((index + 1) * half + index * SMALL_ROWS, SMALL_ROWS), :]
        tables.append(start(source, small.at[vert ^ k], sems.at[at]))
        at += 1
    copies = [start(init_feats.at[span], init_ref.at[vert], sems.at[at])]
    at += 1
    for t in range(tiles):
        target = spread_ref.at[vert * tiles + t, :, pl.ds(0, tile)]
        copies.append(start(tile_vals.at[span, t], target, sems.at[at]))
        at += 1
    for k in range(1, blocks):
        block = vert ^ k
        group, index = ARRIVALS[k]
        base = index * (half + SMALL_ROWS)
        for part, source in ((core, nets[group]), (1 - core, flips[group])):
            first = pl.multiple_of(part * half, half)
            copies.append(
                start(
                    source.at[pl.ds(base, half), pl.ds(0, width)],
                    init_ref.at[block, pl.ds(first, half), :],
                    sems.at[at],
                )
            )
            copies.append(
                start(
                    source.at[pl.ds(base, half), pl.ds(width, tile)],
                    spread_ref.at[block * tiles + part, :, pl.ds(0, tile)],
                    sems.at[at + 1],
                )
            )
            at += 2
    for copy in tables:
        copy.wait()

    owner = core * 4 + zl * 2 + y
    tables = [small[block].astype(jnp.float32) for block in range(blocks)]
    owners = jnp.concatenate([table[0:1, OWNER : OWNER + rows] for table in tables], axis=0)
    cols_out[...] = jnp.concatenate(
        [table[0:1, COLS : COLS + LANES] for table in tables], axis=0
    ).astype(jnp.int32)
    to_scalar = start(cols_out, cols_ref, sems.at[at])
    owned = jnp.where(owners == owner.astype(jnp.float32), 1.0, 0.0)
    earlier = lax.broadcasted_iota(jnp.int32, (rows, rows), 0) < lax.broadcasted_iota(
        jnp.int32, (rows, rows), 1
    )
    rank = jnp.dot(
        owned.astype(jnp.bfloat16),
        jnp.where(earlier, 1.0, 0.0).astype(jnp.bfloat16),
        preferred_element_type=jnp.float32,
    )
    row_ids = lax.broadcasted_iota(jnp.int32, (each, rows), 1).astype(jnp.float32)
    slot_ids = lax.broadcasted_iota(jnp.int32, (slots, rows), 0).astype(jnp.float32)
    for block in range(blocks):
        table = tables[block]
        sends = [
            jnp.where(table[0:each, SEND + peer : SEND + peer + 1] == row_ids, 1.0, 0.0)
            for peer in range(blocks)
        ]
        fills = jnp.where(
            slot_ids == rank[block : block + 1], owned[block : block + 1], 0.0
        )
        pick_ref[block] = jnp.concatenate(sends + [fills], axis=0).astype(jnp.bfloat16)
        live_ref[block * slots : (block + 1) * slots, :] = jnp.broadcast_to(
            jnp.sum(fills, axis=1, keepdims=True), (slots, LANES)
        )
        placing = [
            jnp.where(
                table[0:each, RECV + peer : RECV + peer + 1] == row_ids,
                table[0:each, WEIGHT + peer : WEIGHT + peer + 1],
                0.0,
            )
            for peer in range(blocks)
        ]
        placing = jnp.concatenate(
            placing + [jnp.zeros((LANES - border, rows), jnp.float32)], axis=0
        )
        placing = jnp.transpose(placing).astype(jnp.bfloat16)
        for t in range(tiles):
            spread_ref[block * tiles + t, :, tile : tile + LANES] = placing[
                t * tile : (t + 1) * tile
            ]

    to_scalar.wait()
    for copy in copies:
        copy.wait()
    for block in range(blocks):
        publish(block, init_ref[block], pick_ref, boundary0, keys)
    run_layer(
        spread_ref, cols_ref, init_ref, pick_ref, init_ref, boundary0, weight, mixing_of(0),
        hidden, boundary, anchors,
        pltpu.make_async_copy(weights[0], weight, weight_sems.at[0]).wait,
    )
    loss_ref[...] = score(keys, anchors, live_ref)


def rest_kernel(
    cols_ref, init_ref, spread_ref, pick_ref, live_ref, keys, hidden, boundary,
    loss0_ref, own_ref, flip_ref, even_ref, even_flip_ref, odd_ref, odd_other_ref,
    odd_flip_ref, odd_other_flip_ref, loss_ref, held, border_held, anchors, last, weight,
    weight_sems,
):
    x, core, zl = [lax.axis_index(name) for name in ("x", "core", "zl")]
    layers = SEGMENTS
    blocks = init_ref.shape[0]
    slots = keys.shape[0] // blocks
    half = weight.shape[1] // 2

    def fetch(layer):
        slot, by_x, by_core = layer % 2, layer // 2, layer % 2

        def load(source, part, to):
            first = part * half if isinstance(part, int) else pl.multiple_of(part * half, half)
            pltpu.make_async_copy(
                source, weight.at[slot, pl.ds(first, half), :], weight_sems.at[slot, to]
            ).start()

        def load_whole(source):
            for part in range(2):
                load(source.at[pl.ds(part * half, half), :], part, part)

        near = x == by_x
        pl.when(near & (core == by_core))(lambda: load_whole(own_ref))
        pl.when(near & (core != by_core))(lambda: load_whole(flip_ref))
        if by_core == 0:
            pl.when((x != by_x) & (core == 0))(lambda: load_whole(even_ref))
            pl.when((x != by_x) & (core == 1))(lambda: load_whole(even_flip_ref))
        else:

            @pl.when((x != by_x) & (core == 1))
            def _():
                load(odd_ref, zl, 0)
                load(odd_other_ref, 1 - zl, 1)

            @pl.when((x != by_x) & (core == 0))
            def _():
                load(odd_flip_ref, zl, 0)
                load(odd_other_flip_ref, 1 - zl, 1)

    def arrive(layer):
        slot = layer % 2
        for part in range(2):
            pltpu.make_async_copy(
                own_ref.at[pl.ds(part * half, half), :],
                weight.at[slot, pl.ds(part * half, half), :],
                weight_sems.at[slot, part],
            ).wait()

    fetch(1)

    def report(layer, losses):
        for copy in range(2):
            loss_ref[2 * layer + copy] = losses

    report(0, loss0_ref[...])
    source, border_in = hidden, boundary
    for layer in range(1, layers - 1):
        target, border_out = held.at[layer % 2], border_held.at[layer % 2]
        now, before = anchors.at[layer % 2], anchors.at[1 - layer % 2]

        def meanwhile():
            arrive(layer)
            fetch(layer + 1)
            if layer > 1:
                report(layer - 1, score(keys, before, live_ref))

        run_layer(
            spread_ref, cols_ref, init_ref, pick_ref, source, border_in, weight.at[layer % 2],
            mixing_of(layer), target, border_out, now, meanwhile,
        )
        source, border_in = target, border_out

    border = boundary.shape[1]

    report(layers - 2, score(keys, anchors.at[layers % 2], live_ref))
    for block in range(blocks):
        support = support_of(block, spread_ref, cols_ref, init_ref, source, border_in)
        chosen = jnp.dot(pick_ref[block, border:, :], support, preferred_element_type=jnp.float32)
        last[block * slots : (block + 1) * slots, :] = chosen.astype(jnp.bfloat16)
    arrive(layers - 1)
    final = transform(last[...], weight[(layers - 1) % 2], mixing_of(layers - 1))
    last[...] = rms_unit(final.astype(jnp.float32))
    report(layers - 1, score(keys, last, live_ref))


VMEM = pl.BlockSpec(memory_space=pltpu.VMEM)
SMEM = pl.BlockSpec(memory_space=pltpu.SMEM)
HBM = pl.BlockSpec(memory_space=pltpu.HBM)
FIRST_VMEM = 20 * 1024 * 1024
REST_VMEM = 26 * 1024 * 1024


def local(
    init_feats,
    layer_weight,
    tile_cols,
    tile_vals,
    send_rows,
    send_count,
    recv_rows,
    recv_weight,
    pair_owner,
):
    span_count, rows, width = init_feats.shape
    tile = tile_vals.shape[-1]
    tiles = rows // tile
    blocks = VERTS
    border = blocks * send_rows.shape[-1]
    slots = 3 * rows // (2 * blocks)
    total = blocks * slots
    half = rows // 2
    bf16, f32 = jnp.bfloat16, jnp.float32
    shape = jax.ShapeDtypeStruct
    zh, zl = lax.axis_index("zh"), lax.axis_index("zl")
    own = layer_weight[0]

    packed = shape((half + SMALL_ROWS, width + tile), bf16)
    mine, other = pl.pallas_call(
        pack_kernel,
        out_shape=(packed, packed),
        in_specs=[HBM, HBM] + [VMEM] * 4 + [SMEM, VMEM],
        out_specs=(VMEM, VMEM),
        scratch_shapes=[
            pltpu.VMEM((2, SMALL_ROWS, width + tile), f32),
            pltpu.SemaphoreType.DMA((4,)),
        ],
    )(
        init_feats, tile_vals, send_rows, send_count, recv_rows, recv_weight, tile_cols.T,
        jnp.swapaxes(pair_owner, 1, 2),
    )

    own, mine, other = lax.optimization_barrier((own, mine, other))
    net4, net2, net1 = exchange(other, "zh"), exchange(mine, "zl"), exchange(mine, "y")
    even = exchange(own, "x", core=0)
    odd_part = lax.dynamic_slice(own, (zl * (width // 2), 0), (width // 2, width))
    odd = exchange(odd_part, "x", core=1)
    net4, later = lax.optimization_barrier((net4, own))
    net4, net2 = lax.optimization_barrier((net4, net2))
    net1, net2, net4 = lax.optimization_barrier((net1, net2, net4))
    net6 = exchange(net4, "zl")
    net35 = exchange(jnp.concatenate([net2, net4]), "y")
    net124 = jnp.concatenate([net1, net2, net4])
    flip124 = exchange(net124, "core")
    net7 = exchange(net6, "y")
    flip = exchange(own, "core")
    net35, flip124, net6, odd, even = lax.optimization_barrier((net35, flip124, net6, odd, even))
    flip35, flip6 = exchange(net35, "core"), exchange(net6, "core")
    even_flip = exchange(even, "core", core=0)
    odd_other = exchange(odd, "zl", core=1)
    net7, flip35, flip6, even_flip = lax.optimization_barrier((net7, flip35, flip6, even_flip))
    flip7 = exchange(net7, "core")
    odd, odd_other, flip7 = lax.optimization_barrier((odd, odd_other, flip7))
    odd_flip = exchange(odd, "core", core=1)
    odd_other_flip = exchange(odd_other, "core", core=1)

    keep = [
        shape((blocks, rows, width), bf16),
        shape((blocks * tiles, tile, tile + LANES), bf16),
        shape((blocks, border + slots, rows), bf16),
        shape((blocks, LANES), jnp.int32),
        shape((total, LANES), f32),
        shape((total, width), bf16),
        shape((blocks, rows, width), bf16),
        shape((blocks, border, width), f32),
        shape((1, total), f32),
    ]
    init, spread, pick, cols, live, keys, hidden, boundary, loss0 = pl.pallas_call(
        first_kernel,
        out_shape=keep,
        in_specs=[HBM] * 15,
        out_specs=[VMEM] * len(keep),
        scratch_shapes=[
            pltpu.VMEM((blocks, border, width), f32),
            pltpu.VMEM((total, width), bf16),
            pltpu.VMEM((blocks, SMALL_ROWS, width + tile), bf16),
            pltpu.VMEM((width, width), bf16),
            pltpu.SMEM((blocks, LANES), jnp.int32),
            pltpu.SemaphoreType.DMA((8 * blocks,)),
            pltpu.SemaphoreType.DMA((1,)),
        ],
        compiler_params=pltpu.CompilerParams(vmem_limit_bytes=FIRST_VMEM),
        cost_estimate=pl.CostEstimate(
            flops=2 * blocks * rows * width * width, bytes_accessed=1 << 24, transcendentals=0
        ),
    )(
        init_feats, tile_vals, mine, net124, net35, net6, net7, flip124, flip35, flip6, flip7,
        own, flip, even, even_flip,
    )
    losses = pl.pallas_call(
        rest_kernel,
        out_shape=shape((2 * SEGMENTS, 1, total), f32),
        in_specs=[SMEM] + [VMEM] * 8 + [HBM] * 8,
        out_specs=VMEM,
        scratch_shapes=[
            pltpu.VMEM((2, blocks, rows, width), bf16),
            pltpu.VMEM((2, blocks, border, width), f32),
            pltpu.VMEM((2, total, width), bf16),
            pltpu.VMEM((total, width), bf16),
            pltpu.VMEM((2, width, width), bf16),
            pltpu.SemaphoreType.DMA((2, 2)),
        ],
        compiler_params=pltpu.CompilerParams(vmem_limit_bytes=REST_VMEM),
        cost_estimate=pl.CostEstimate(
            flops=6 * blocks * rows * width * width, bytes_accessed=1 << 24, transcendentals=0
        ),
    )(
        cols, init, spread, pick, live, keys, hidden, boundary, loss0, own, flip, even,
        even_flip, odd, odd_other, odd_flip, odd_other_flip,
    )
    losses = lax.all_to_all(losses, ("x", "core", "zh"), split_axis=0, concat_axis=0, tiled=True)
    losses = lax.dynamic_index_in_dim(
        losses.reshape(2, 2, 2, total), zh, axis=1, keepdims=False
    )
    return jnp.swapaxes(losses, 0, 1).reshape(1, span_count, total)


def from_behind(block, axis, distance):
    devices = range(lax.axis_size(axis))
    route = [(i - distance, i) for i in devices if i - distance in devices]
    return lax.ppermute(block, axis, route)


def rms_rows(vectors):
    vectors = vectors.astype(jnp.float32)
    return (
        vectors * lax.rsqrt(jnp.mean(vectors * vectors, axis=-1, keepdims=True) + 1e-06)
    ).astype(jnp.bfloat16)


def pack_pairs(owners, embed, init_span, capacity, vert_count):
    row_count = embed.shape[0]
    target_dev = owners[:, 0]
    onehot = (target_dev[:, None] == jnp.arange(vert_count)[None, :]).astype(jnp.int32)
    before = jnp.cumsum(onehot, axis=0) - onehot
    place = jnp.sum(before * onehot, axis=1)
    lookup = (
        jnp.full((vert_count * capacity,), row_count, jnp.int32)
        .at[target_dev * capacity + place]
        .set(jnp.arange(row_count, dtype=jnp.int32))
    )
    blank = jnp.zeros((1, embed.shape[1]), jnp.bfloat16)
    padded_embed = jnp.concatenate([embed, blank], axis=0)
    padded_init = jnp.concatenate([init_span, blank], axis=0)
    anchors = padded_embed[lookup].reshape(vert_count, capacity, -1)
    keys_all = padded_init[lookup].reshape(vert_count, capacity, -1)
    flags = (lookup < row_count).astype(jnp.bfloat16).reshape(vert_count, capacity)
    return (anchors, keys_all, flags)


def score_pairs(anchors, keys_all, flags):
    feature_columns = anchors.shape[-1]
    query_rows = rms_rows(anchors.reshape(-1, feature_columns))
    normalized_keys = rms_rows(keys_all.reshape(-1, feature_columns))
    similarity_scores = jnp.dot(
        query_rows, normalized_keys.T, preferred_element_type=jnp.float32
    ) / (feature_columns * SOFTMAX_TEMP)
    live_mask = flags.reshape(-1).astype(jnp.float32)
    totals = jnp.sum(jnp.exp(similarity_scores) * live_mask[None, :], axis=1)
    diagonal = jnp.diagonal(similarity_scores)
    return (jnp.log(totals + 1.0 - live_mask) - diagonal) * live_mask


def local_by_section(
    init_feats,
    layer_weight,
    tile_cols,
    tile_vals,
    send_rows,
    send_count,
    recv_rows,
    recv_weight,
    pair_owner,
):
    segment_count = lax.axis_size("segment")
    vert_count = lax.axis_size("vert")
    position = lax.axis_index("segment")
    span_count, row_count, feature_columns = init_feats.shape
    capacity = 3 * row_count // (2 * vert_count)
    tile_size = tile_vals.shape[-1]
    tile_rows = row_count // tile_size
    slot_count = send_rows.shape[-1]
    weight = layer_weight[0]
    mixing = jnp.log(LAMBDA_DECAY / (position.astype(jnp.float32) + 1.0) + 1.0)
    row_ids = jnp.arange(row_count, dtype=jnp.int32)

    def section(span_id, hidden, init_span):
        columns = tile_cols[span_id]
        values = tile_vals[span_id]
        picked = hidden.reshape(tile_rows, tile_size, feature_columns)[columns]
        local_sum = jnp.einsum(
            "tij,tjd->tid", values, picked, preferred_element_type=jnp.float32
        ).reshape(row_count, feature_columns)
        retain = jnp.arange(slot_count)[None, :] < send_count[span_id][:, None]
        outgoing = jnp.where(
            retain[..., None], hidden[send_rows[span_id]], jnp.zeros((), jnp.bfloat16)
        )
        incoming = lax.all_to_all(outgoing, "vert", split_axis=0, concat_axis=0, tiled=True)
        targets = recv_rows[span_id].reshape(-1)
        edge_weights = recv_weight[span_id].reshape(-1)
        placing = jnp.where(
            targets[None, :] == row_ids[:, None], edge_weights[None, :], jnp.zeros((), jnp.bfloat16)
        )
        border = jnp.dot(
            placing, incoming.reshape(-1, feature_columns), preferred_element_type=jnp.float32
        )
        mixed = (1.0 - ALPHA_MIX) * (local_sum + border) + ALPHA_MIX * init_span.astype(jnp.float32)
        support = mixed.astype(jnp.bfloat16)
        product = jnp.dot(support, weight, preferred_element_type=jnp.float32)
        return jax.nn.relu((1.0 - mixing) * support.astype(jnp.float32) + mixing * product).astype(
            jnp.bfloat16
        )

    stored = jnp.zeros((span_count, row_count, feature_columns), jnp.bfloat16)

    def advance(moment, carry):
        arrived, stored_now = carry
        span_raw = moment - position
        active = (span_raw >= 0) & (span_raw < span_count)
        span_id = jnp.clip(span_raw, 0, span_count - 1)
        init_span = init_feats[span_id]
        hidden = jnp.where(position == 0, init_span, arrived)
        result = section(span_id, hidden, init_span)
        passed = from_behind(result, "segment", 1)
        stored_now = jnp.where(active, stored_now.at[span_id].set(result), stored_now)
        return (passed, stored_now)

    start_carry = (jnp.zeros((row_count, feature_columns), jnp.bfloat16), stored)
    final_carry = lax.fori_loop(0, span_count + segment_count - 1, advance, start_carry)
    stored = final_carry[1]

    def pack_one(owners, embed, init_span):
        return pack_pairs(owners, embed, init_span, capacity, vert_count)

    anchors, keys_all, flags = jax.vmap(pack_one)(pair_owner, stored, init_feats)
    got_anchors, got_keys, got_flags = (
        lax.all_to_all(anchors, "vert", split_axis=1, concat_axis=1, tiled=True),
        lax.all_to_all(keys_all, "vert", split_axis=1, concat_axis=1, tiled=True),
        lax.all_to_all(flags, "vert", split_axis=1, concat_axis=1, tiled=True),
    )
    losses = jax.vmap(score_pairs)(got_anchors, got_keys, got_flags)
    return losses[None]


def solution(mesh):
    specs = (
        P(None, "vert", None),
        P("segment", None, None),
        P(None, "vert"),
        P(None, "vert", None, None),
        P(None, "vert", None),
        P(None, "vert"),
        P(None, "vert", None),
        P(None, "vert", None),
        P(None, "vert", None),
    )
    out_spec = P("segment", None, "vert")
    if (mesh.shape["segment"], mesh.shape["vert"]) != (SEGMENTS, VERTS):
        return jax.shard_map(
            local_by_section, mesh=mesh, in_specs=specs, out_specs=out_spec, check_vma=False
        )
    parts = {"segment": AXES[:2], "vert": AXES[2:], None: None}
    fine = Mesh(mesh.devices.reshape((2,) * len(AXES)), AXES)

    def split(spec):
        return P(*[parts[name] for name in spec])

    return jax.shard_map(
        local,
        mesh=fine,
        in_specs=tuple(split(spec) for spec in specs),
        out_specs=split(out_spec),
        check_vma=False,
    )
```

```python
import functools
import itertools

import jax
import jax.numpy as jnp
import numpy as np
from jax import lax
from jax.experimental import pallas as pl
from jax.experimental.pallas import tpu as pltpu
from jax.sharding import Mesh
from jax.sharding import PartitionSpec as P

ALPHA_MIX = 0.5
LAMBDA_DECAY = 0.5
SOFTMAX_TEMP = 0.1
NORM_EPS = 1e-06

AXES = ("x", "core", "zh", "zl", "y")
SPANS, SEGMENTS, VERTS = 4, 4, 8
SMALL_ROWS = 16
LANES = 128
SEND, RECV, WEIGHT, COLS, OWNER = 0, 128, 256, 512, 640


ARRIVALS = {1: (0, 0), 2: (0, 1), 4: (0, 2), 3: (1, 0), 5: (1, 1), 6: (2, 0), 7: (3, 0)}


def exchange(block, *across, core=None):
    sizes = [range(lax.axis_size(name)) for name in AXES]
    pairs = []
    for index, here in enumerate(itertools.product(*sizes)):
        there = [1 - at if name in across else at for name, at in zip(AXES, here, strict=True)]
        target = functools.reduce(lambda total, digit: total * 2 + digit, there, 0)
        if core is None or here[1] == core:
            pairs.append((index, target))
    return lax.ppermute(block, AXES, pairs)


def rms_unit(vectors):
    scale = lax.rsqrt(jnp.mean(vectors * vectors, axis=-1, keepdims=True) + NORM_EPS)
    return (vectors * scale).astype(jnp.bfloat16)


def mixing_of(layer):
    return float(np.log(np.float32(LAMBDA_DECAY) / np.float32(layer + 1) + np.float32(1.0)))


def turned(matrix):
    rows, columns = matrix.shape
    whole = jnp.concatenate([matrix, jnp.zeros((rows, LANES - columns), matrix.dtype)], axis=1)
    return jnp.transpose(whole)[:columns]


def pack_kernel(
    init_ref, tiles_ref, send_ref, count_ref, recv_ref, weight_ref, cols_ref, owner_ref,
    mine_ref, other_ref, small, sems,
):
    x, core, zh = [lax.axis_index(name) for name in AXES[:3]]
    half, width = mine_ref.shape[0] - SMALL_ROWS, init_ref.shape[-1]
    peers, slots = send_ref.shape[1:]
    tiles, rows = cols_ref.shape[0], owner_ref.shape[-1]
    lane = lax.broadcasted_iota(jnp.int32, (1, LANES), 1)
    first = pl.multiple_of(core * half, half)
    spans = (zh * 2 + x, (1 - zh) * 2 + x)
    copies = []
    for i, out_ref in enumerate((mine_ref, other_ref)):
        copies.append(
            pltpu.make_async_copy(
                init_ref.at[spans[i], pl.ds(first, half), :],
                out_ref.at[pl.ds(0, half), pl.ds(0, width)],
                sems.at[2 * i],
            )
        )
        copies.append(
            pltpu.make_async_copy(
                tiles_ref.at[spans[i], core],
                out_ref.at[pl.ds(0, half), pl.ds(width, half)],
                sems.at[2 * i + 1],
            )
        )
    for copy in copies:
        copy.start()
    small[...] = jnp.zeros_like(small)
    for i, out_ref in enumerate((mine_ref, other_ref)):
        span = spans[i]
        sends = turned(send_ref[span].astype(jnp.float32))
        used = lax.broadcasted_iota(jnp.int32, (slots, peers), 0) < count_ref[pl.ds(span, 1), :]
        small[i, 0:slots, SEND : SEND + peers] = jnp.where(used, sends, float(rows))
        small[i, 0:slots, RECV : RECV + peers] = turned(recv_ref[span].astype(jnp.float32))
        small[i, 0:slots, WEIGHT : WEIGHT + peers] = turned(weight_ref[span].astype(jnp.float32))
        columns = jnp.zeros((1, LANES), jnp.int32)
        for t in range(tiles):
            columns = jnp.where(lane == t, cols_ref[t, span], columns)
        small[i, 0:1, COLS : COLS + LANES] = columns.astype(jnp.float32)
        small[i, 0:1, OWNER : OWNER + rows] = owner_ref[span].astype(jnp.float32)
        out_ref[half : half + SMALL_ROWS, :] = small[i].astype(jnp.bfloat16)
    for copy in copies:
        copy.wait()


def support_of(block, spread_ref, cols_ref, init_ref, hidden, boundary):
    tile = spread_ref.shape[1]
    rows = init_ref.shape[1]
    incoming = boundary[block].astype(jnp.bfloat16)
    depth = tile + incoming.shape[0]
    parts = []
    for t in range(rows // tile):
        column = cols_ref[block, t]
        start = pl.multiple_of(column * tile, tile)
        source = jnp.concatenate([hidden[block, pl.ds(start, tile), :], incoming], axis=0)
        gathered = jnp.dot(
            spread_ref[block * (rows // tile) + t, :, 0:depth],
            source,
            preferred_element_type=jnp.float32,
        )
        init = init_ref[block, t * tile : (t + 1) * tile, :].astype(jnp.float32)
        parts.append(((1.0 - ALPHA_MIX) * gathered + ALPHA_MIX * init).astype(jnp.bfloat16))
    return jnp.concatenate(parts, axis=0)


def transform(support, weight, mixing):
    product = jnp.dot(support, weight, preferred_element_type=jnp.float32)
    blended = (1.0 - mixing) * support.astype(jnp.float32) + mixing * product
    return jnp.maximum(blended, 0.0).astype(jnp.bfloat16)


def publish(block, block_out, pick_ref, boundary, target):
    receivers, border, _ = boundary.shape
    each = border // receivers
    picked = jnp.dot(pick_ref[block], block_out, preferred_element_type=jnp.float32)
    border_start = pl.multiple_of(block * each, each)
    for receiver in range(receivers):
        boundary[receiver, pl.ds(border_start, each), :] = picked[
            receiver * each : (receiver + 1) * each
        ]
    slots = target.shape[0] // receivers
    slot_start = pl.multiple_of(block * slots, slots)
    target[pl.ds(slot_start, slots), :] = rms_unit(picked[border:])


def score(keys, anchors, live_ref):
    total, width = keys.shape
    logits = lax.dot_general(
        keys[...], anchors[...], (((1,), (1,)), ((), ())), preferred_element_type=jnp.float32
    ) / (width * SOFTMAX_TEMP)
    live = live_ref[:, 0:1]
    key_ids = lax.broadcasted_iota(jnp.int32, (total, total), 0)
    anchor_ids = lax.broadcasted_iota(jnp.int32, (total, total), 1)
    same = key_ids == anchor_ids
    live_row = jnp.sum(jnp.where(same, live, 0.0), axis=0, keepdims=True)
    totals = jnp.sum(jnp.exp(logits) * live, axis=0, keepdims=True)
    diagonal = jnp.sum(jnp.where(same, logits, 0.0), axis=0, keepdims=True)
    return (jnp.log(totals + 1.0 - live_row) - diagonal) * live_row


def run_layer(spread_ref, cols_ref, init_ref, pick_ref, source, border_in, weight, mixing,
              target, border_out, anchors, meanwhile, group=2):
    blocks, rows, _ = init_ref.shape
    for first in range(0, blocks, group):
        support = jnp.concatenate(
            [
                support_of(first + k, spread_ref, cols_ref, init_ref, source, border_in)
                for k in range(group)
            ],
            axis=0,
        )
        if first == 0:
            meanwhile()
        out = transform(support, weight[...], mixing)
        for k in range(group):
            block_out = out[k * rows : (k + 1) * rows]
            target[first + k] = block_out
            publish(first + k, block_out, pick_ref, border_out, anchors)


def first_kernel(
    init_feats, tile_vals, mine_ref, *rest
):
    blocks = VERTS
    nets, flips, weights = rest[:4], rest[4:8], rest[8:12]
    (init_ref, spread_ref, pick_ref, cols_out, live_ref, keys, hidden, boundary, loss_ref,
     boundary0, anchors, small, weight, cols_ref, sems, weight_sems) = rest[12:]
    x, core, zh, zl, y = [lax.axis_index(name) for name in AXES]
    vert = zh * 4 + zl * 2 + y
    rows, width = init_ref.shape[1:]
    half = rows // 2
    tile = spread_ref.shape[1]
    tiles = rows // tile
    border = boundary.shape[1]
    each = border // blocks
    slots = keys.shape[0] // blocks

    def start(source, target, sem):
        copy = pltpu.make_async_copy(source, target, sem)
        copy.start()
        return copy

    for place, source in enumerate(weights):
        by_x, by_core = place // 2, place % 2

        @pl.when((x == by_x) & (core == by_core))
        def _():
            pltpu.make_async_copy(source, weight, weight_sems.at[0]).start()

    span = zh * 2 + x
    tables = [start(mine_ref.at[pl.ds(half, SMALL_ROWS), :], small.at[vert], sems.at[0])]
    at = 1
    for k in range(1, blocks):
        group, index = ARRIVALS[k]
        source = nets[group].at[pl.ds((index + 1) * half + index * SMALL_ROWS, SMALL_ROWS), :]
        tables.append(start(source, small.at[vert ^ k], sems.at[at]))
        at += 1
    copies = [start(init_feats.at[span], init_ref.at[vert], sems.at[at])]
    at += 1
    for t in range(tiles):
        target = spread_ref.at[vert * tiles + t, :, pl.ds(0, tile)]
        copies.append(start(tile_vals.at[span, t], target, sems.at[at]))
        at += 1
    for k in range(1, blocks):
        block = vert ^ k
        group, index = ARRIVALS[k]
        base = index * (half + SMALL_ROWS)
        for part, source in ((core, nets[group]), (1 - core, flips[group])):
            first = pl.multiple_of(part * half, half)
            copies.append(
                start(
                    source.at[pl.ds(base, half), pl.ds(0, width)],
                    init_ref.at[block, pl.ds(first, half), :],
                    sems.at[at],
                )
            )
            copies.append(
                start(
                    source.at[pl.ds(base, half), pl.ds(width, tile)],
                    spread_ref.at[block * tiles + part, :, pl.ds(0, tile)],
                    sems.at[at + 1],
                )
            )
            at += 2
    for copy in tables + copies:
        copy.wait()

    owner = core * 4 + zl * 2 + y
    tables = [small[block].astype(jnp.float32) for block in range(blocks)]
    owners = jnp.concatenate([table[0:1, OWNER : OWNER + rows] for table in tables], axis=0)
    cols_out[...] = jnp.concatenate(
        [table[0:1, COLS : COLS + LANES] for table in tables], axis=0
    ).astype(jnp.int32)
    to_scalar = start(cols_out, cols_ref, sems.at[at])
    owned = jnp.where(owners == owner.astype(jnp.float32), 1.0, 0.0)
    earlier = lax.broadcasted_iota(jnp.int32, (rows, rows), 0) < lax.broadcasted_iota(
        jnp.int32, (rows, rows), 1
    )
    rank = jnp.dot(
        owned.astype(jnp.bfloat16),
        jnp.where(earlier, 1.0, 0.0).astype(jnp.bfloat16),
        preferred_element_type=jnp.float32,
    )
    row_ids = lax.broadcasted_iota(jnp.int32, (each, rows), 1).astype(jnp.float32)
    slot_ids = lax.broadcasted_iota(jnp.int32, (slots, rows), 0).astype(jnp.float32)
    for block in range(blocks):
        table = tables[block]
        sends = [
            jnp.where(table[0:each, SEND + peer : SEND + peer + 1] == row_ids, 1.0, 0.0)
            for peer in range(blocks)
        ]
        fills = jnp.where(
            slot_ids == rank[block : block + 1], owned[block : block + 1], 0.0
        )
        pick_ref[block] = jnp.concatenate(sends + [fills], axis=0).astype(jnp.bfloat16)
        live_ref[block * slots : (block + 1) * slots, :] = jnp.broadcast_to(
            jnp.sum(fills, axis=1, keepdims=True), (slots, LANES)
        )
        placing = [
            jnp.where(
                table[0:each, RECV + peer : RECV + peer + 1] == row_ids,
                table[0:each, WEIGHT + peer : WEIGHT + peer + 1],
                0.0,
            )
            for peer in range(blocks)
        ]
        placing = jnp.concatenate(
            placing + [jnp.zeros((LANES - border, rows), jnp.float32)], axis=0
        )
        placing = jnp.transpose(placing).astype(jnp.bfloat16)
        for t in range(tiles):
            spread_ref[block * tiles + t, :, tile : tile + LANES] = placing[
                t * tile : (t + 1) * tile
            ]

    def begin(block, carry):
        publish(block, init_ref[block], pick_ref, boundary0, keys)
        return carry

    lax.fori_loop(0, blocks, begin, 0, unroll=4)
    to_scalar.wait()
    pltpu.make_async_copy(weights[0], weight, weight_sems.at[0]).wait()
    run_layer(
        spread_ref, cols_ref, init_ref, pick_ref, init_ref, boundary0, weight, mixing_of(0),
        hidden, boundary, anchors, lambda: None,
    )
    loss_ref[...] = score(keys, anchors, live_ref)


def rest_kernel(
    cols_ref, init_ref, spread_ref, pick_ref, live_ref, keys, hidden, boundary,
    loss0_ref, own_ref, flip_ref, even_ref, even_flip_ref, odd_ref, odd_other_ref,
    odd_flip_ref, odd_other_flip_ref, loss_ref, held, border_held, anchors, last, weight,
    weight_sems,
):
    x, core, zl = [lax.axis_index(name) for name in ("x", "core", "zl")]
    layers = SEGMENTS
    blocks = init_ref.shape[0]
    slots = keys.shape[0] // blocks
    half = weight.shape[1] // 2

    def fetch(layer):
        slot, by_x, by_core = layer % 2, layer // 2, layer % 2

        def load(source, part, to):
            first = part * half if isinstance(part, int) else pl.multiple_of(part * half, half)
            pltpu.make_async_copy(
                source, weight.at[slot, pl.ds(first, half), :], weight_sems.at[slot, to]
            ).start()

        def load_whole(source):
            for part in range(2):
                load(source.at[pl.ds(part * half, half), :], part, part)

        near = x == by_x
        pl.when(near & (core == by_core))(lambda: load_whole(own_ref))
        pl.when(near & (core != by_core))(lambda: load_whole(flip_ref))
        if by_core == 0:
            pl.when((x != by_x) & (core == 0))(lambda: load_whole(even_ref))
            pl.when((x != by_x) & (core == 1))(lambda: load_whole(even_flip_ref))
        else:

            @pl.when((x != by_x) & (core == 1))
            def _():
                load(odd_ref, zl, 0)
                load(odd_other_ref, 1 - zl, 1)

            @pl.when((x != by_x) & (core == 0))
            def _():
                load(odd_flip_ref, zl, 0)
                load(odd_other_flip_ref, 1 - zl, 1)

    def arrive(layer):
        slot = layer % 2
        for part in range(2):
            pltpu.make_async_copy(
                own_ref.at[pl.ds(part * half, half), :],
                weight.at[slot, pl.ds(part * half, half), :],
                weight_sems.at[slot, part],
            ).wait()

    fetch(1)

    def report(layer, losses):
        for copy in range(2):
            loss_ref[2 * layer + copy] = losses

    report(0, loss0_ref[...])
    source, border_in = hidden, boundary
    for layer in range(1, layers - 1):
        target, border_out = held.at[layer % 2], border_held.at[layer % 2]
        now, before = anchors.at[layer % 2], anchors.at[1 - layer % 2]

        def meanwhile():
            arrive(layer)
            fetch(layer + 1)
            if layer > 1:
                report(layer - 1, score(keys, before, live_ref))

        run_layer(
            spread_ref, cols_ref, init_ref, pick_ref, source, border_in, weight.at[layer % 2],
            mixing_of(layer), target, border_out, now, meanwhile,
        )
        source, border_in = target, border_out

    border = boundary.shape[1]

    report(layers - 2, score(keys, anchors.at[layers % 2], live_ref))
    for block in range(blocks):
        support = support_of(block, spread_ref, cols_ref, init_ref, source, border_in)
        chosen = jnp.dot(pick_ref[block, border:, :], support, preferred_element_type=jnp.float32)
        last[block * slots : (block + 1) * slots, :] = chosen.astype(jnp.bfloat16)
    arrive(layers - 1)
    final = transform(last[...], weight[(layers - 1) % 2], mixing_of(layers - 1))
    last[...] = rms_unit(final.astype(jnp.float32))
    report(layers - 1, score(keys, last, live_ref))


VMEM = pl.BlockSpec(memory_space=pltpu.VMEM)
SMEM = pl.BlockSpec(memory_space=pltpu.SMEM)
HBM = pl.BlockSpec(memory_space=pltpu.HBM)
FIRST_VMEM = 20 * 1024 * 1024
REST_VMEM = 26 * 1024 * 1024


def local(
    init_feats,
    layer_weight,
    tile_cols,
    tile_vals,
    send_rows,
    send_count,
    recv_rows,
    recv_weight,
    pair_owner,
):
    span_count, rows, width = init_feats.shape
    tile = tile_vals.shape[-1]
    tiles = rows // tile
    blocks = VERTS
    border = blocks * send_rows.shape[-1]
    slots = 3 * rows // (2 * blocks)
    total = blocks * slots
    half = rows // 2
    bf16, f32 = jnp.bfloat16, jnp.float32
    shape = jax.ShapeDtypeStruct
    zh, zl = lax.axis_index("zh"), lax.axis_index("zl")
    own = layer_weight[0]

    packed = shape((half + SMALL_ROWS, width + tile), bf16)
    mine, other = pl.pallas_call(
        pack_kernel,
        out_shape=(packed, packed),
        in_specs=[HBM, HBM] + [VMEM] * 4 + [SMEM, VMEM],
        out_specs=(VMEM, VMEM),
        scratch_shapes=[
            pltpu.VMEM((2, SMALL_ROWS, width + tile), f32),
            pltpu.SemaphoreType.DMA((4,)),
        ],
    )(
        init_feats, tile_vals, send_rows, send_count, recv_rows, recv_weight, tile_cols.T,
        jnp.swapaxes(pair_owner, 1, 2),
    )

    own, mine, other = lax.optimization_barrier((own, mine, other))
    net4, net2, net1 = exchange(other, "zh"), exchange(mine, "zl"), exchange(mine, "y")
    even = exchange(own, "x", core=0)
    odd_part = lax.dynamic_slice(own, (zl * (width // 2), 0), (width // 2, width))
    odd = exchange(odd_part, "x", core=1)
    net4, later = lax.optimization_barrier((net4, own))
    net4, net2 = lax.optimization_barrier((net4, net2))
    net1, net2, net4 = lax.optimization_barrier((net1, net2, net4))
    net6 = exchange(net4, "zl")
    net35 = exchange(jnp.concatenate([net2, net4]), "y")
    net124 = jnp.concatenate([net1, net2, net4])
    flip124 = exchange(net124, "core")
    net7 = exchange(net6, "y")
    flip = exchange(own, "core")
    net35, flip124, net6, odd, even = lax.optimization_barrier((net35, flip124, net6, odd, even))
    flip35, flip6 = exchange(net35, "core"), exchange(net6, "core")
    even_flip = exchange(even, "core", core=0)
    odd_other = exchange(odd, "zl", core=1)
    net7, flip35, flip6, even_flip = lax.optimization_barrier((net7, flip35, flip6, even_flip))
    flip7 = exchange(net7, "core")
    odd, odd_other, flip7 = lax.optimization_barrier((odd, odd_other, flip7))
    odd_flip = exchange(odd, "core", core=1)
    odd_other_flip = exchange(odd_other, "core", core=1)

    keep = [
        shape((blocks, rows, width), bf16),
        shape((blocks * tiles, tile, tile + LANES), bf16),
        shape((blocks, border + slots, rows), bf16),
        shape((blocks, LANES), jnp.int32),
        shape((total, LANES), f32),
        shape((total, width), bf16),
        shape((blocks, rows, width), bf16),
        shape((blocks, border, width), f32),
        shape((1, total), f32),
    ]
    init, spread, pick, cols, live, keys, hidden, boundary, loss0 = pl.pallas_call(
        first_kernel,
        out_shape=keep,
        in_specs=[HBM] * 15,
        out_specs=[VMEM] * len(keep),
        scratch_shapes=[
            pltpu.VMEM((blocks, border, width), f32),
            pltpu.VMEM((total, width), bf16),
            pltpu.VMEM((blocks, SMALL_ROWS, width + tile), bf16),
            pltpu.VMEM((width, width), bf16),
            pltpu.SMEM((blocks, LANES), jnp.int32),
            pltpu.SemaphoreType.DMA((8 * blocks,)),
            pltpu.SemaphoreType.DMA((1,)),
        ],
        compiler_params=pltpu.CompilerParams(vmem_limit_bytes=FIRST_VMEM),
        cost_estimate=pl.CostEstimate(
            flops=2 * blocks * rows * width * width, bytes_accessed=1 << 24, transcendentals=0
        ),
    )(
        init_feats, tile_vals, mine, net124, net35, net6, net7, flip124, flip35, flip6, flip7,
        own, flip, even, even_flip,
    )
    losses = pl.pallas_call(
        rest_kernel,
        out_shape=shape((2 * SEGMENTS, 1, total), f32),
        in_specs=[SMEM] + [VMEM] * 8 + [HBM] * 8,
        out_specs=VMEM,
        scratch_shapes=[
            pltpu.VMEM((2, blocks, rows, width), bf16),
            pltpu.VMEM((2, blocks, border, width), f32),
            pltpu.VMEM((2, total, width), bf16),
            pltpu.VMEM((total, width), bf16),
            pltpu.VMEM((2, width, width), bf16),
            pltpu.SemaphoreType.DMA((2, 2)),
        ],
        compiler_params=pltpu.CompilerParams(vmem_limit_bytes=REST_VMEM),
        cost_estimate=pl.CostEstimate(
            flops=6 * blocks * rows * width * width, bytes_accessed=1 << 24, transcendentals=0
        ),
    )(
        cols, init, spread, pick, live, keys, hidden, boundary, loss0, own, flip, even,
        even_flip, odd, odd_other, odd_flip, odd_other_flip,
    )
    losses = lax.all_to_all(losses, ("x", "core", "zh"), split_axis=0, concat_axis=0, tiled=True)
    losses = lax.dynamic_index_in_dim(
        losses.reshape(2, 2, 2, total), zh, axis=1, keepdims=False
    )
    return jnp.swapaxes(losses, 0, 1).reshape(1, span_count, total)


def from_behind(block, axis, distance):
    devices = range(lax.axis_size(axis))
    route = [(i - distance, i) for i in devices if i - distance in devices]
    return lax.ppermute(block, axis, route)


def rms_rows(vectors):
    vectors = vectors.astype(jnp.float32)
    return (
        vectors * lax.rsqrt(jnp.mean(vectors * vectors, axis=-1, keepdims=True) + 1e-06)
    ).astype(jnp.bfloat16)


def pack_pairs(owners, embed, init_span, capacity, vert_count):
    row_count = embed.shape[0]
    target_dev = owners[:, 0]
    onehot = (target_dev[:, None] == jnp.arange(vert_count)[None, :]).astype(jnp.int32)
    before = jnp.cumsum(onehot, axis=0) - onehot
    place = jnp.sum(before * onehot, axis=1)
    lookup = (
        jnp.full((vert_count * capacity,), row_count, jnp.int32)
        .at[target_dev * capacity + place]
        .set(jnp.arange(row_count, dtype=jnp.int32))
    )
    blank = jnp.zeros((1, embed.shape[1]), jnp.bfloat16)
    padded_embed = jnp.concatenate([embed, blank], axis=0)
    padded_init = jnp.concatenate([init_span, blank], axis=0)
    anchors = padded_embed[lookup].reshape(vert_count, capacity, -1)
    keys_all = padded_init[lookup].reshape(vert_count, capacity, -1)
    flags = (lookup < row_count).astype(jnp.bfloat16).reshape(vert_count, capacity)
    return (anchors, keys_all, flags)


def score_pairs(anchors, keys_all, flags):
    feature_columns = anchors.shape[-1]
    query_rows = rms_rows(anchors.reshape(-1, feature_columns))
    normalized_keys = rms_rows(keys_all.reshape(-1, feature_columns))
    similarity_scores = jnp.dot(
        query_rows, normalized_keys.T, preferred_element_type=jnp.float32
    ) / (feature_columns * SOFTMAX_TEMP)
    live_mask = flags.reshape(-1).astype(jnp.float32)
    totals = jnp.sum(jnp.exp(similarity_scores) * live_mask[None, :], axis=1)
    diagonal = jnp.diagonal(similarity_scores)
    return (jnp.log(totals + 1.0 - live_mask) - diagonal) * live_mask


def local_by_section(
    init_feats,
    layer_weight,
    tile_cols,
    tile_vals,
    send_rows,
    send_count,
    recv_rows,
    recv_weight,
    pair_owner,
):
    segment_count = lax.axis_size("segment")
    vert_count = lax.axis_size("vert")
    position = lax.axis_index("segment")
    span_count, row_count, feature_columns = init_feats.shape
    capacity = 3 * row_count // (2 * vert_count)
    tile_size = tile_vals.shape[-1]
    tile_rows = row_count // tile_size
    slot_count = send_rows.shape[-1]
    weight = layer_weight[0]
    mixing = jnp.log(LAMBDA_DECAY / (position.astype(jnp.float32) + 1.0) + 1.0)
    row_ids = jnp.arange(row_count, dtype=jnp.int32)

    def section(span_id, hidden, init_span):
        columns = tile_cols[span_id]
        values = tile_vals[span_id]
        picked = hidden.reshape(tile_rows, tile_size, feature_columns)[columns]
        local_sum = jnp.einsum(
            "tij,tjd->tid", values, picked, preferred_element_type=jnp.float32
        ).reshape(row_count, feature_columns)
        retain = jnp.arange(slot_count)[None, :] < send_count[span_id][:, None]
        outgoing = jnp.where(
            retain[..., None], hidden[send_rows[span_id]], jnp.zeros((), jnp.bfloat16)
        )
        incoming = lax.all_to_all(outgoing, "vert", split_axis=0, concat_axis=0, tiled=True)
        targets = recv_rows[span_id].reshape(-1)
        edge_weights = recv_weight[span_id].reshape(-1)
        placing = jnp.where(
            targets[None, :] == row_ids[:, None], edge_weights[None, :], jnp.zeros((), jnp.bfloat16)
        )
        border = jnp.dot(
            placing, incoming.reshape(-1, feature_columns), preferred_element_type=jnp.float32
        )
        mixed = (1.0 - ALPHA_MIX) * (local_sum + border) + ALPHA_MIX * init_span.astype(jnp.float32)
        support = mixed.astype(jnp.bfloat16)
        product = jnp.dot(support, weight, preferred_element_type=jnp.float32)
        return jax.nn.relu((1.0 - mixing) * support.astype(jnp.float32) + mixing * product).astype(
            jnp.bfloat16
        )

    stored = jnp.zeros((span_count, row_count, feature_columns), jnp.bfloat16)

    def advance(moment, carry):
        arrived, stored_now = carry
        span_raw = moment - position
        active = (span_raw >= 0) & (span_raw < span_count)
        span_id = jnp.clip(span_raw, 0, span_count - 1)
        init_span = init_feats[span_id]
        hidden = jnp.where(position == 0, init_span, arrived)
        result = section(span_id, hidden, init_span)
        passed = from_behind(result, "segment", 1)
        stored_now = jnp.where(active, stored_now.at[span_id].set(result), stored_now)
        return (passed, stored_now)

    start_carry = (jnp.zeros((row_count, feature_columns), jnp.bfloat16), stored)
    final_carry = lax.fori_loop(0, span_count + segment_count - 1, advance, start_carry)
    stored = final_carry[1]

    def pack_one(owners, embed, init_span):
        return pack_pairs(owners, embed, init_span, capacity, vert_count)

    anchors, keys_all, flags = jax.vmap(pack_one)(pair_owner, stored, init_feats)
    got_anchors, got_keys, got_flags = (
        lax.all_to_all(anchors, "vert", split_axis=1, concat_axis=1, tiled=True),
        lax.all_to_all(keys_all, "vert", split_axis=1, concat_axis=1, tiled=True),
        lax.all_to_all(flags, "vert", split_axis=1, concat_axis=1, tiled=True),
    )
    losses = jax.vmap(score_pairs)(got_anchors, got_keys, got_flags)
    return losses[None]


def solution(mesh):
    specs = (
        P(None, "vert", None),
        P("segment", None, None),
        P(None, "vert"),
        P(None, "vert", None, None),
        P(None, "vert", None),
        P(None, "vert"),
        P(None, "vert", None),
        P(None, "vert", None),
        P(None, "vert", None),
    )
    out_spec = P("segment", None, "vert")
    if (mesh.shape["segment"], mesh.shape["vert"]) != (SEGMENTS, VERTS):
        return jax.shard_map(
            local_by_section, mesh=mesh, in_specs=specs, out_specs=out_spec, check_vma=False
        )
    parts = {"segment": AXES[:2], "vert": AXES[2:], None: None}
    fine = Mesh(mesh.devices.reshape((2,) * len(AXES)), AXES)

    def split(spec):
        return P(*[parts[name] for name in spec])

    return jax.shard_map(
        local,
        mesh=fine,
        in_specs=tuple(split(spec) for spec in specs),
        out_specs=split(out_spec),
        check_vma=False,
    )
```
